512 devices in a mesh: scen: 2 (over core), wide: 64 (over y, z), blk: 4 (over x).
Axes of the slice: x: 4, y: 8, z: 8, core: 2. Of those that a mesh axis runs over, the one named last changes fastest.
Arguments:
- weather: bfloat16 [8192, 128], P('scen'), parts along dimension 0, may hold values from -6 to 6
- response: bfloat16 [8192, 64, 128], P('wide', 'blk'), may hold values from -0.0625 to 0.0625
- coupling: bfloat16 [64, 2, 128, 128], P('wide'), may hold values from -0.375 to 0.375
- sources: int32 [64, 2], replicated, may hold values from 0 to 63
- delays: int32 [64, 2], replicated, may hold values from 1 to 16, as said below
Outputs:
- temps: bfloat16 [16384, 4096], P(('scen', 'wide'), 'blk'), parts along dimension 0
The draws below stay inside these ranges and needn't reach their ends.
There are 2 independent parts, one for each index of `scen`. The reference program is written for one: setup_inputs(seed, part) draws one part's arguments, and reference() takes and returns one part's arrays. A program takes and returns all parts, laid end to end along the dimension named above; an argument that names none is the same for every part. Nothing has to cross between parts.
Inputs may be any that keep to these rules, and one draw needn't show every extreme that they name: `delays`: delay of each edge in steps; some edge has delay 16.
All inputs are finite; a program needn't handle non-finite values.
Results may differ from the reference program's by a relative error of at most 0.0085.
Values may be sent and summed in bfloat16 or wider, within the bound.
A program may use at most 64 MiB of HBM per device.

```python
import math
import jax
import jax.numpy as jnp
from jax import lax

CH = 128
LAGS = 64
BS = 128
DEG = 2
MAXDELAY = 16
NODE_BLOCKS = 64
NODES = 8192
TIME = 4096


def draw_delays(key, part):
    key = jax.random.fold_in(key, 7)
    first_key, second_key = jax.random.split(key)
    values = jax.random.randint(first_key, (NODE_BLOCKS * DEG,), 1, MAXDELAY + 1)
    where_most = jax.random.randint(second_key, (), 0, NODE_BLOCKS * DEG)
    values = jnp.where(jnp.arange(NODE_BLOCKS * DEG) == where_most, MAXDELAY, values)
    return values.reshape(NODE_BLOCKS, DEG).astype(jnp.int32)


def set_ends(array, stream_key, least, largest):
    longest = array.shape.index(max(array.shape))
    spots = []
    for shift in (0, 1):
        where = [jax.random.randint(jax.random.fold_in(stream_key, axis), (), 0, length) for axis, length in enumerate(array.shape)]
        where[longest] = (where[longest] + shift) % array.shape[longest]
        spots.append(tuple(where))
    return array.at[spots[0]].set(least).at[spots[1]].set(largest)


def level_of(key, shape, pieces, low, high):
    def one(dim, parts):
        steps = jax.random.uniform(jax.random.fold_in(jax.random.fold_in(key, 6), dim), (parts,), jnp.float32, low / len(pieces), high / len(pieces))
        return jnp.repeat(jnp.exp(steps), shape[dim] // parts).reshape((-1,) + (1,) * (len(shape) - dim - 1))

    factor_of = one(*pieces[0])
    for cut in pieces[1:]:
        factor_of = factor_of * one(*cut)
    return factor_of


def normal_values(own_key, extent, deviation, bound, cuts=(), held_as=jnp.bfloat16):
    values = jax.random.normal(own_key, extent, jnp.float32) * deviation
    if len(cuts) > 0:
        values = level_of(own_key, extent, cuts, -0.22, 0.18) * values
    return jnp.clip(values, min=-bound, max=bound).astype(held_as)


def setup_inputs(seed: int = 0, part: int = 0) -> dict:
    key_list = jax.random.split(jax.random.key(seed), 6)
    own_keys = jax.random.split(jax.random.fold_in(key_list[5], part), 6)
    return {
        "weather": normal_values(own_keys[0], (TIME, CH), 1.0, 6.0),
        "response": normal_values(key_list[1], (NODES, LAGS, CH), (LAGS * CH) ** -0.5, 0.0625, ((0, 64), (1, 4))),
        "coupling": normal_values(key_list[2], (NODE_BLOCKS, DEG, BS, BS), (BS * DEG) ** -0.5, 0.375, ((0, 64),)),
        "sources": set_ends(jax.random.randint(key_list[3], (NODE_BLOCKS, DEG), 0, NODE_BLOCKS), jax.random.fold_in(key_list[3], 1), 0, NODE_BLOCKS - 1).astype(jnp.int32),
        "delays": draw_delays(jax.random.fold_in(key_list[5], 71), part),
    }


def transport(series, coupling, sources, delays):
    total = series.shape[0]
    padded = jnp.pad(series, ((MAXDELAY, 0), (0, 0))).reshape(total + MAXDELAY, NODE_BLOCKS, BS)

    def one_block(block_index):
        upstream = jnp.take(padded, sources[block_index], axis=1)
        upstream = jnp.transpose(upstream, (1, 0, 2))

        def cut_series(single, lag_value):
            return lax.dynamic_slice_in_dim(single, (MAXDELAY - lag_value).astype(jnp.int32), total, 0)

        moved = jax.vmap(cut_series)(upstream, delays[block_index])
        return jnp.einsum("etb,ebc->tc", moved.astype(jnp.float32), coupling[block_index].astype(jnp.float32))

    carried = lax.map(one_block, jnp.arange(NODE_BLOCKS, dtype=jnp.int32))
    carried = jnp.transpose(carried, (1, 0, 2)).reshape(total, NODES)
    return series.astype(jnp.float32) + carried


def reference(weather, response, coupling, sources, delays):
    block_rows = math.gcd(TIME, 512)
    padded_drive = jnp.pad(weather, ((LAGS - 1, 0), (0, 0)))
    kernel_matrix = response.reshape(NODES, LAGS * CH)

    def demand_block(first_row):
        window = lax.dynamic_slice_in_dim(padded_drive, first_row, block_rows + LAGS - 1, 0)
        lagged = jnp.stack([window[LAGS - 1 - lag_index:LAGS - 1 - lag_index + block_rows] for lag_index in range(LAGS)], axis=1)
        lagged = lagged.reshape(block_rows, LAGS * CH)
        return lax.dot_general(lagged, kernel_matrix, (((1,), (1,)), ((), ())), preferred_element_type=jnp.float32)

    starts = jnp.arange(TIME // block_rows, dtype=jnp.int32) * block_rows
    demand = lax.map(demand_block, starts).reshape(TIME, NODES)
    load = demand.astype(jnp.bfloat16)
    first = transport(load, coupling, sources, delays).astype(jnp.bfloat16)
    second = transport(first, coupling, sources, delays).astype(jnp.bfloat16)
    return jnp.transpose(second)
```

```python
import functools

import jax
import jax.numpy as jnp
from jax import lax
from jax.experimental import pallas as pl
from jax.experimental.pallas import tpu as pltpu
from jax.sharding import PartitionSpec as P

MESH = pl.DeviceIdType.MESH
CH = 128
LAGS = 64
BS = 128
HALO = 16
RING = 8
BLOCKS = 64
HALF = 32
ROWS = 32
QUARTER = HALF * ROWS
EXT = QUARTER + 2 * HALO
LROWS = ROWS + 2 * HALO
FROWS = ROWS + HALO
PIECE = 4
PARTS = 4
GROUP = 16
XROWS = EXT + LAGS - GROUP
WPRE = 96
TILE = 352


def drain(ref, sem):
    pltpu.make_async_copy(ref, ref, sem).wait()


def kernel(
    weather,
    resp,
    coupling,
    sources,
    delays,
    out,
    wraw,
    w32,
    xbuf,
    rbuf,
    acc,
    lext,
    lbuf,
    l32,
    fbuf,
    f32b,
    sbuf,
    cown,
    cmir,
    loc_sem,
    own_sem,
    self_sem,
    a_send,
    a_recv,
    am_send,
    am_recv,
    c1_send,
    c1_recv,
    c2_send,
    c2_recv,
    cm_send,
    cm_recv,
    b_send,
    b_recv,
    bm_send,
    bm_recv,
    f_send,
    f_recv,
    e_send,
    e_recv,
):
    s = lax.axis_index("scen")
    w = lax.axis_index("wide")
    x = lax.axis_index("blk")
    y, z = w // RING, w % RING
    first_core = s == 0
    u = jnp.where(first_core, z, y)
    v = jnp.where(first_core, y, z)
    right, left = (x + 1) % PARTS, (x + PARTS - 1) % PARTS
    far = (x + 2) % PARTS

    def wide_of(uu, vv):
        return jnp.where(first_core, vv * RING + uu, uu * RING + vv)

    def remote(src, dst, send, recv, core, wide, blk):
        return pltpu.make_async_remote_copy(
            src_ref=src,
            dst_ref=dst,
            send_sem=send,
            recv_sem=recv,
            device_id=(core, wide, blk),
            device_id_type=MESH,
        )

    sister = (1 - s, w, x)
    core_t = w // HALF
    slot = w % HALF
    own_target = core_t == s

    lead = pl.multiple_of(jnp.maximum(x * QUARTER - WPRE, 0), 32)
    here = pl.multiple_of(x * QUARTER, QUARTER)
    main_copy = pltpu.make_async_copy(
        weather.at[pl.ds(here, QUARTER)], wraw.at[pl.ds(WPRE, QUARTER)], loc_sem.at[0]
    )
    lead_copy = pltpu.make_async_copy(
        weather.at[pl.ds(lead, WPRE)], wraw.at[pl.ds(0, WPRE)], loc_sem.at[1]
    )
    resp_copy = pltpu.make_async_copy(resp, rbuf.at[pl.ds(4 * x, 4)], own_sem.at[0])
    coup_copy = pltpu.make_async_copy(coupling.at[0, s], cown.at[v * RING + u], own_sem.at[1])
    main_copy.start()
    lead_copy.start()
    resp_copy.start()
    coup_copy.start()

    barrier = pltpu.get_barrier_semaphore()

    def greet(core, wide, blk):
        pl.semaphore_signal(barrier, inc=1, device_id=(core, wide, blk), device_id_type=MESH)

    greet(s, w, right)
    greet(s, w, left)
    greet(*sister)

    @pl.loop(1, RING)
    def _(step):
        greet(s, wide_of((u + step) % RING, v), x)

    greet(s, wide_of(u, (v + 1) % RING), x)
    greet(s, wide_of(u, (v + RING - 1) % RING), x)

    @pl.loop(1, HALF)
    def _(step):
        greet(core_t, HALF * s + (slot + step) % HALF, x)

    @pl.when(jnp.logical_not(own_target))
    def _():
        greet(core_t, HALF * s + slot, x)

    pl.semaphore_wait(barrier, 3 + RING - 1 + 2 + HALF - 1 + jnp.where(own_target, 0, 1))

    def a_copy(index, src, piece, blk):
        return remote(src, rbuf.at[piece], a_send.at[index], a_recv.at[index], s, w, blk)

    p0, p1 = 2 * s, 2 * s + 1
    a_copies = [
        a_copy(0, resp.at[p0], 4 * x + p0, right),
        a_copy(1, resp.at[p1], 4 * x + p1, left),
        a_copy(2, resp.at[p1], 4 * x + p1, right),
        a_copy(3, resp.at[p0], 4 * x + p0, left),
    ]
    for copy in a_copies:
        copy.start()

    own_row = v * RING + u

    @pl.loop(1, RING)
    def _(step):
        remote(
            coupling.at[0, s],
            cown.at[own_row],
            c1_send,
            c1_recv,
            s,
            wide_of((u + step) % RING, v),
            x,
        ).start()

    main_copy.wait()
    lead_copy.wait()

    @pl.when(x == 0)
    def _():
        wraw[pl.ds(0, WPRE), :] = jnp.zeros((WPRE, CH), jnp.bfloat16)

    w32[...] = wraw[...].astype(jnp.float32)
    for lag in range(GROUP):
        xbuf[:, lag * CH : (lag + 1) * CH] = w32[GROUP - lag : GROUP - lag + XROWS, :].astype(
            jnp.bfloat16
        )

    def add_group(group, first):
        base = (LAGS - GROUP) - GROUP * group

        @pl.loop(0, EXT // TILE)
        def _(tile):
            row = pl.multiple_of(tile * TILE, 16)
            start = pl.multiple_of(base + row, 16)
            total = None
            for piece in range(4):
                term = lax.dot_general(
                    xbuf[pl.ds(start, TILE), piece * PIECE * CH : (piece + 1) * PIECE * CH],
                    rbuf[4 * group + piece],
                    (((1,), (1,)), ((), ())),
                    preferred_element_type=jnp.float32,
                )
                total = term if total is None else total + term
            if not first:
                total = total + acc[pl.ds(row, TILE), :]
            acc[pl.ds(row, TILE), :] = total

    resp_copy.wait()
    add_group(x, True)

    def mirror_piece(piece, group_sem):
        remote(
            rbuf.at[piece], rbuf.at[piece], am_send, am_recv.at[group_sem], *sister
        ).start()

    a_copies[0].wait_recv()
    fwd_right = a_copy(4, rbuf.at[4 * left + p0], 4 * left + p0, right)
    fwd_right.start()
    mirror_piece(4 * left + p0, 0)
    a_copies[1].wait_recv()
    fwd_left = a_copy(5, rbuf.at[4 * right + p1], 4 * right + p1, left)
    fwd_left.start()
    mirror_piece(4 * right + p1, 1)

    coup_copy.wait()
    drain(cown.at[pl.ds(0, RING - 1)], c1_recv)

    def needed(row, half):
        return jnp.where(first_core, row // 4 == 1, half == 0)

    def c_chunk(row, half):
        return cown.at[pl.ds(row * RING + 4 * half, 4)]

    def c_mirror(row, half):
        @pl.when(needed(row, half))
        def _():
            remote(
                c_chunk(row, half),
                cmir.at[pl.ds(row * RING + 4 * half, 4)],
                cm_send,
                cm_recv,
                *sister,
            ).start()

    def c_step(way, step, half):
        if way == 0:
            row, to = (v + RING - step + 1) % RING, (v + 1) % RING
        else:
            row, to = (v + step - 1) % RING, (v + RING - 1) % RING
        index = (way * 4 + step - 1) * 2 + half
        return remote(
            c_chunk(row, half),
            c_chunk(row, half),
            c2_send,
            c2_recv.at[index],
            s,
            wide_of(u, to),
            x,
        )

    def c_start(step):
        for half in range(2):
            for way in range(2):
                if step < 4 or half == way:
                    c_step(way, step, half).start()

    def c_arrive(step):
        for half in range(2):
            for way in range(2):
                if step < 4 or half == way:
                    c_step(way, step, half).wait_recv()
                    if step < 3 or (step == 3 and half == way):
                        c_step(way, step + 1, half).start()
                    row = (v + RING - step) % RING if way == 0 else (v + step) % RING
                    c_mirror(row, half)

    c_start(1)
    c_mirror(v, 0)
    c_mirror(v, 1)

    a_copies[2].wait_recv()
    mirror_piece(4 * left + p1, 0)
    a_copies[3].wait_recv()
    mirror_piece(4 * right + p0, 1)
    c_arrive(1)
    fwd_right.wait_recv()
    mirror_piece(4 * far + p0, 2)
    fwd_left.wait_recv()
    mirror_piece(4 * far + p1, 2)
    drain(rbuf.at[pl.ds(0, 2)], am_recv.at[0])
    add_group(left, False)
    drain(rbuf.at[pl.ds(0, 2)], am_recv.at[1])
    add_group(right, False)
    drain(rbuf.at[pl.ds(0, 2)], am_recv.at[2])
    add_group(far, False)
    lext[...] = acc[...].astype(jnp.bfloat16)

    def b_copy(i):
        return remote(
            lext.at[pl.ds(pl.multiple_of(ROWS * i, ROWS), LROWS)],
            lbuf.at[w],
            b_send,
            b_recv.at[slot // 8],
            core_t,
            HALF * s + i,
            x,
        )

    def b_local():
        return pltpu.make_async_copy(
            lext.at[pl.ds(pl.multiple_of(ROWS * slot, ROWS), LROWS)], lbuf.at[w], b_recv.at[slot // 8]
        )

    @pl.loop(1, HALF)
    def _(step):
        b_copy((slot + step) % HALF).start()

    @pl.when(own_target)
    def _():
        b_local().start()

    @pl.when(jnp.logical_not(own_target))
    def _():
        b_copy(slot).start()

    c_arrive(2)
    c_arrive(3)

    mine = HALF * s
    theirs = HALF * (1 - s)

    def mirror(buf, first, count, send, recv):
        part = buf.at[pl.ds(first, count)]
        return remote(part, part, send, recv, *sister)

    for part in range(4):
        drain(lbuf.at[pl.ds(0, 8)], b_recv.at[part])
        mirror(lbuf, mine + 8 * part, 8, bm_send, bm_recv.at[part]).start()
        l32[pl.ds(mine + 8 * part, 8)] = lbuf[pl.ds(mine + 8 * part, 8)].astype(jnp.float32)
    c_arrive(4)
    for part in range(4):
        drain(lbuf.at[pl.ds(0, 8)], bm_recv.at[part])
        l32[pl.ds(theirs + 8 * part, 8)] = lbuf[pl.ds(theirs + 8 * part, 8)].astype(jnp.float32)
    drain(cmir.at[pl.ds(0, HALF)], cm_recv)

    def moved(series, i, start, rows):
        a = series[sources[i, s], pl.ds(start - delays[i, s], rows), :]
        b = series[sources[i, 1 - s], pl.ds(start - delays[i, 1 - s], rows), :]
        lhs = jnp.concatenate([a, b], axis=1).astype(jnp.bfloat16)
        turned = (i % RING) * RING + i // RING
        rhs = jnp.concatenate(
            [cown[jnp.where(first_core, i, turned)], cmir[jnp.where(first_core, turned, i)]], axis=0
        )
        return jnp.dot(lhs, rhs, preferred_element_type=jnp.float32)

    for part in range(4):

        @pl.loop(0, 8, unroll=4)
        def _(m):
            i = mine + 8 * part + m
            total = l32[i, HALO:LROWS, :] + moved(l32, i, HALO, FROWS)
            rounded = total.astype(jnp.bfloat16)
            fbuf[i] = rounded
            f32b[i] = rounded.astype(jnp.float32)

        mirror(fbuf, mine + 8 * part, 8, f_send, f_recv.at[part]).start()

    for part in range(4):
        drain(fbuf.at[pl.ds(0, 8)], f_recv.at[part])
        f32b[pl.ds(theirs + 8 * part, 8)] = fbuf[pl.ds(theirs + 8 * part, 8)].astype(jnp.float32)

    span = pl.ds(pl.multiple_of(ROWS * slot, ROWS), ROWS)

    def second(m):
        i = mine + m
        total = f32b[i, HALO:FROWS, :] + moved(f32b, i, HALO, ROWS)
        sbuf[m] = total.astype(jnp.bfloat16)

    def e_copy(m):
        return remote(sbuf.at[m], out.at[span], e_send, e_recv, core_t, mine + m, x)

    def e_local():
        return pltpu.make_async_copy(sbuf.at[slot], out.at[span], e_recv)

    second(slot)

    @pl.when(own_target)
    def _():
        e_local().start()

    @pl.when(jnp.logical_not(own_target))
    def _():
        e_copy(slot).start()

    @pl.loop(1, HALF)
    def _(step):
        m = (slot + step) % HALF
        second(m)
        e_copy(m).start()

    drain(out, e_recv)
    for copy in a_copies + [fwd_right, fwd_left]:
        copy.wait_send()
    drain(rbuf.at[pl.ds(0, 6)], am_send)
    drain(cown.at[pl.ds(0, RING - 1)], c1_send)
    drain(cown.at[pl.ds(0, 56)], c2_send)
    drain(cmir.at[pl.ds(0, HALF)], cm_send)
    drain(lbuf.at[pl.ds(0, HALF - 1)], b_send)
    drain(sbuf.at[pl.ds(0, HALF - 1)], e_send)

    @pl.when(jnp.logical_not(own_target))
    def _():
        drain(lbuf.at[0], b_send)
        drain(sbuf.at[0], e_send)

    drain(lbuf.at[pl.ds(0, HALF)], bm_send)
    drain(fbuf.at[pl.ds(0, HALF)], f_send)


def body(weather, response, coupling, sources, delays):
    pieces = response.reshape(BS, 4, PIECE * CH).transpose(1, 0, 2)
    bf16, f32 = jnp.bfloat16, jnp.float32
    vm, dma = pltpu.VMEM, pltpu.SemaphoreType.DMA
    rows = pl.pallas_call(
        kernel,
        out_shape=jax.ShapeDtypeStruct((QUARTER, BS), bf16),
        in_specs=[pl.BlockSpec(memory_space=pl.ANY)] * 3
        + [pl.BlockSpec(memory_space=pltpu.SMEM)] * 2,
        out_specs=pl.BlockSpec(memory_space=pl.ANY),
        scratch_shapes=[
            vm((WPRE + QUARTER, CH), bf16),
            vm((WPRE + QUARTER, CH), f32),
            vm((XROWS, GROUP * CH), bf16),
            vm((16, BS, PIECE * CH), bf16),
            vm((EXT, BS), f32),
            vm((EXT, BS), bf16),
            vm((BLOCKS, LROWS, BS), bf16),
            vm((BLOCKS, LROWS, BS), f32),
            vm((BLOCKS, FROWS, BS), bf16),
            vm((BLOCKS, FROWS, BS), f32),
            vm((HALF, ROWS, BS), bf16),
            vm((BLOCKS, BS, BS), bf16),
            vm((BLOCKS, BS, BS), bf16),
            dma((2,)),
            dma((2,)),
            dma,
            dma((6,)),
            dma((6,)),
            dma,
            dma((3,)),
            dma,
            dma,
            dma,
            dma((16,)),
            dma,
            dma,
            dma,
            dma((4,)),
            dma,
            dma((4,)),
            dma,
            dma((4,)),
            dma,
            dma,
        ],
        compiler_params=pltpu.CompilerParams(
            collective_id=0, has_side_effects=True, vmem_limit_bytes=40 * 1024 * 1024
        ),
    )(weather, pieces, coupling, sources, delays)
    return rows.T


def solution(mesh):
    placed = (P("scen", None), P("wide", "blk", None), P("wide", None, None, None), P(), P())
    return jax.shard_map(
        body, mesh=mesh, in_specs=placed, out_specs=P(("scen", "wide"), "blk"), check_vma=False
    )
```

```python
import functools

import jax
import jax.numpy as jnp
from jax import lax
from jax.experimental import pallas as pl
from jax.experimental.pallas import tpu as pltpu
from jax.sharding import PartitionSpec as P

MESH = pl.DeviceIdType.MESH
CH = 128
LAGS = 64
BS = 128
HALO = 16
RING = 8
BLOCKS = 64
HALF = 32
ROWS = 32
QUARTER = HALF * ROWS
EXT = QUARTER + 2 * HALO
LROWS = ROWS + 2 * HALO
FROWS = ROWS + HALO
PIECE = 4
PARTS = 4
GROUP = 16
XROWS = EXT + LAGS - GROUP
WPRE = 96
TILE = 352
STRIDE = 5


def drain(ref, sem):
    pltpu.make_async_copy(ref, ref, sem).wait()


def kernel(
    weather,
    resp,
    coupling,
    sources,
    delays,
    out,
    rraw,
    r32,
    wraw,
    w32,
    xbuf,
    rbuf,
    acc,
    lext,
    lbuf,
    l32,
    fbuf,
    f32b,
    sbuf,
    cown,
    loc_sem,
    own_sem,
    a_send,
    a_recv,
    am_send,
    am_recv,
    c1_send,
    c1_recv,
    c2_send,
    c2_recv,
    b_send,
    b_recv,
    bm_send,
    bm_recv,
    f_send,
    f_recv,
    e_send,
    e_recv,
):
    s = lax.axis_index("scen")
    w = lax.axis_index("wide")
    x = lax.axis_index("blk")
    y, z = w // RING, w % RING
    first_core = s == 0
    u = jnp.where(first_core, z, y)
    v = jnp.where(first_core, y, z)
    right, left = (x + 1) % PARTS, (x + PARTS - 1) % PARTS
    far = (x + 2) % PARTS

    def wide_of(uu, vv):
        return jnp.where(first_core, vv * RING + uu, uu * RING + vv)

    def remote(src, dst, send, recv, core, wide, blk):
        return pltpu.make_async_remote_copy(
            src_ref=src,
            dst_ref=dst,
            send_sem=send,
            recv_sem=recv,
            device_id=(core, wide, blk),
            device_id_type=MESH,
        )

    sister = (1 - s, w, x)
    core_t = (y + z) % 2
    slot = w // 2

    def chip(core, m):
        return 2 * m + (core + m // 4) % 2

    own_target = core_t == s

    lead = pl.multiple_of(jnp.maximum(x * QUARTER - WPRE, 0), 32)
    here = pl.multiple_of(x * QUARTER, QUARTER)
    main_copy = pltpu.make_async_copy(
        weather.at[pl.ds(here, QUARTER)], wraw.at[pl.ds(WPRE, QUARTER)], loc_sem.at[0]
    )
    lead_copy = pltpu.make_async_copy(
        weather.at[pl.ds(lead, WPRE)], wraw.at[pl.ds(0, WPRE)], loc_sem.at[1]
    )
    resp_copy = pltpu.make_async_copy(resp, rraw, own_sem)
    resp_copy.start()
    main_copy.start()
    lead_copy.start()

    barrier = pltpu.get_barrier_semaphore()

    def greet(core, wide, blk):
        pl.semaphore_signal(barrier, inc=1, device_id=(core, wide, blk), device_id_type=MESH)

    greet(s, w, right)
    greet(s, w, left)
    greet(*sister)

    @pl.loop(1, RING)
    def _(step):
        greet(s, wide_of((u + step) % RING, v), x)

    greet(s, wide_of(u, (v + 1) % RING), x)
    greet(s, wide_of(u, (v + RING - 1) % RING), x)

    @pl.loop(1, HALF)
    def _(step):
        greet(core_t, chip(s, (slot + step) % HALF), x)

    @pl.when(jnp.logical_not(own_target))
    def _():
        greet(core_t, chip(s, slot), x)

    def lay_out(core):
        for lag in range(GROUP // 2):
            column = (lag % PIECE) * CH
            rbuf[4 * x + 2 * core + lag // PIECE, :, column : column + CH] = r32[
                pl.ds(GROUP // 2 * core + lag, BS, stride=GROUP), :
            ].astype(jnp.bfloat16)

    resp_copy.wait()
    r32[...] = rraw[...].astype(jnp.float32)
    lay_out(s)

    pl.semaphore_wait(barrier, 3 + RING - 1 + 2 + HALF - 1 + jnp.where(own_target, 0, 1))

    def a_copy(index, src, piece, blk):
        return remote(src, rbuf.at[piece], a_send.at[index], a_recv.at[index], s, w, blk)

    p0, p1 = 2 * s, 2 * s + 1
    a_copies = [
        a_copy(0, rbuf.at[4 * x + p0], 4 * x + p0, right),
        a_copy(1, rbuf.at[4 * x + p1], 4 * x + p1, left),
        a_copy(2, rbuf.at[4 * x + p1], 4 * x + p1, right),
        a_copy(3, rbuf.at[4 * x + p0], 4 * x + p0, left),
    ]
    for copy in a_copies:
        copy.start()

    @pl.when(own_target)
    def _():
        pltpu.make_async_copy(coupling.at[0], cown.at[4 * v], c1_recv.at[0]).start()
        for away, place in ((1, 1), (7, 0), (2, 2), (6, 1), (3, 3), (5, 2), (4, 3)):
            remote(
                coupling.at[0],
                cown.at[4 * v + place],
                c1_send,
                c1_recv.at[place],
                s,
                wide_of((u + away) % RING, v),
                x,
            ).start()

    def c_step(way, step, piece):
        if way == 0:
            row, to = (v + RING - step + 1) % RING, (v + 1) % RING
        else:
            row, to = (v + step - 1) % RING, (v + RING - 1) % RING
        part = cown.at[4 * row + piece]
        index = (way * 4 + step - 1) * 4 + piece
        return remote(part, part, c2_send, c2_recv.at[index], s, wide_of(u, to), x)

    def goes(way, step, piece):
        return step < 4 or (step == 4 and piece // 2 == way)

    def c_begin(*pieces):
        for piece in pieces:
            drain(cown.at[0], c1_recv.at[piece])
            for way in range(2):
                c_step(way, 1, piece).start()

    def c_arrive(step, *pieces):
        for piece in pieces:
            for way in range(2):
                if goes(way, step, piece):
                    c_step(way, step, piece).wait_recv()
                    if goes(way, step + 1, piece):
                        c_step(way, step + 1, piece).start()

    main_copy.wait()
    lead_copy.wait()

    @pl.when(x == 0)
    def _():
        wraw[pl.ds(0, WPRE), :] = jnp.zeros((WPRE, CH), jnp.bfloat16)

    w32[...] = wraw[...].astype(jnp.float32)
    for lag in range(GROUP):
        xbuf[:, lag * CH : (lag + 1) * CH] = w32[GROUP - lag : GROUP - lag + XROWS, :].astype(
            jnp.bfloat16
        )

    def add_groups(groups, tile, first=False):
        total = None if first else acc[pl.ds(tile * TILE, TILE), :]
        for group in groups:
            start = pl.multiple_of((LAGS - GROUP) - GROUP * group + tile * TILE, 16)
            for piece in range(4):
                term = lax.dot_general(
                    xbuf[pl.ds(start, TILE), piece * PIECE * CH : (piece + 1) * PIECE * CH],
                    rbuf[4 * group + piece],
                    (((1,), (1,)), ((), ())),
                    preferred_element_type=jnp.float32,
                )
                total = term if total is None else total + term
        return total

    def keep(tile, total):
        acc[pl.ds(tile * TILE, TILE), :] = total

    lay_out(1 - s)
    c_begin(0)
    for tile in range(3):
        keep(tile, add_groups([x], tile, True))

    def mirror_piece(piece, group_sem):
        remote(
            rbuf.at[piece], rbuf.at[piece], am_send, am_recv.at[group_sem], *sister
        ).start()

    a_copies[0].wait_recv()
    fwd_right = a_copy(4, rbuf.at[4 * left + p0], 4 * left + p0, right)
    fwd_right.start()
    a_copies[1].wait_recv()
    fwd_left = a_copy(5, rbuf.at[4 * right + p1], 4 * right + p1, left)
    fwd_left.start()
    mirror_piece(4 * left + p0, 0)
    mirror_piece(4 * right + p1, 1)

    c_begin(1, 2, 3)

    c_arrive(1, 0)
    a_copies[2].wait_recv()
    mirror_piece(4 * left + p1, 0)
    a_copies[3].wait_recv()
    mirror_piece(4 * right + p0, 1)
    c_arrive(1, 1, 2)
    drain(rbuf.at[pl.ds(0, 2)], am_recv.at[0])
    drain(rbuf.at[pl.ds(0, 2)], am_recv.at[1])
    keep(0, add_groups([left, right], 0))
    c_arrive(1, 3)
    keep(1, add_groups([left, right], 1))
    c_arrive(2, 0)
    fwd_right.wait_recv()
    mirror_piece(4 * far + p0, 2)
    fwd_left.wait_recv()
    mirror_piece(4 * far + p1, 2)
    keep(2, add_groups([left, right], 2))
    c_arrive(2, 1, 2)
    drain(rbuf.at[pl.ds(0, 2)], am_recv.at[2])
    for tile in range(3):
        lext[pl.ds(tile * TILE, TILE), :] = add_groups([far], tile).astype(jnp.bfloat16)

    def b_copy(i):
        return remote(
            lext.at[pl.ds(pl.multiple_of(ROWS * i, ROWS), LROWS)],
            lbuf.at[HALF * core_t + slot],
            b_send,
            b_recv.at[slot // 8],
            core_t,
            chip(s, i),
            x,
        )

    def b_local():
        return pltpu.make_async_copy(
            lext.at[pl.ds(pl.multiple_of(ROWS * slot, ROWS), LROWS)], lbuf.at[HALF * core_t + slot], b_recv.at[slot // 8]
        )

    @pl.loop(1, HALF)
    def _(step):
        b_copy((slot + STRIDE * step) % HALF).start()

    @pl.when(own_target)
    def _():
        b_local().start()

    @pl.when(jnp.logical_not(own_target))
    def _():
        b_copy(slot).start()

    c_arrive(2, 3)
    c_arrive(3, 0, 1, 2, 3)
    c_arrive(4, 0, 2, 1, 3)

    mine = HALF * s
    theirs = HALF * (1 - s)

    def mirror(buf, first, count, send, recv):
        part = buf.at[pl.ds(first, count)]
        return remote(part, part, send, recv, *sister)

    for part in range(4):
        drain(lbuf.at[pl.ds(0, 8)], b_recv.at[part])
        mirror(lbuf, mine + 8 * part, 8, bm_send, bm_recv.at[part]).start()
        l32[pl.ds(mine + 8 * part, 8)] = lbuf[pl.ds(mine + 8 * part, 8)].astype(jnp.float32)
    for part in range(4):
        drain(lbuf.at[pl.ds(0, 8)], bm_recv.at[part])
        l32[pl.ds(theirs + 8 * part, 8)] = lbuf[pl.ds(theirs + 8 * part, 8)].astype(jnp.float32)

    def block_of(wide):
        return HALF * ((wide // RING + wide) % 2) + wide // 2

    def moved(series, m, start, rows):
        wide = chip(s, m)
        upstream = [
            series[block_of(sources[k, wide]), pl.ds(start - delays[k, wide], rows), :]
            for k in range(2)
        ]
        lhs = jnp.concatenate(upstream, axis=1).astype(jnp.bfloat16)
        wy, wz = wide // RING, wide % RING
        row = jnp.where(first_core, wy, wz)
        away = (jnp.where(first_core, wz, wy) - u + RING) % RING
        place = jnp.where(
            away % 2 == 0,
            jnp.where(away == 0, 0, jnp.where(away == 2, 1, jnp.where(away == 6, 2, 3))),
            jnp.where(away == 1, 0, jnp.where(away == 7, 1, jnp.where(away == 3, 2, 3))),
        )
        rhs = cown[4 * row + place].reshape(2 * BS, BS)
        return jnp.dot(lhs, rhs, preferred_element_type=jnp.float32)

    for part in range(4):

        @pl.loop(0, 8, unroll=8)
        def _(m):
            i = mine + 8 * part + m
            total = l32[i, HALO:LROWS, :] + moved(l32, 8 * part + m, HALO, FROWS)
            rounded = total.astype(jnp.bfloat16)
            fbuf[i] = rounded
            f32b[i] = rounded.astype(jnp.float32)

        mirror(fbuf, mine + 8 * part, 8, f_send, f_recv.at[part]).start()

    for part in range(4):
        drain(fbuf.at[pl.ds(0, 8)], f_recv.at[part])
        f32b[pl.ds(theirs + 8 * part, 8)] = fbuf[pl.ds(theirs + 8 * part, 8)].astype(jnp.float32)

    span = pl.ds(pl.multiple_of(ROWS * slot, ROWS), ROWS)

    def second(m):
        i = mine + m
        total = f32b[i, HALO:FROWS, :] + moved(f32b, m, HALO, ROWS)
        sbuf[m] = total.astype(jnp.bfloat16)

    def e_copy(m):
        return remote(sbuf.at[m], out.at[span], e_send, e_recv, core_t, chip(s, m), x)

    def e_local():
        return pltpu.make_async_copy(sbuf.at[slot], out.at[span], e_recv)

    second(slot)

    @pl.when(own_target)
    def _():
        e_local().start()

    @pl.when(jnp.logical_not(own_target))
    def _():
        e_copy(slot).start()

    def second_batch(first, count):
        picked = [(slot + first + k) % HALF for k in range(count)]
        for m in picked:
            second(m)
        for m in picked:
            e_copy(m).start()

    second_batch(1, 3)

    @pl.loop(1, 8)
    def _(batch):
        second_batch(4 * batch, 4)

    drain(out, e_recv)
    for copy in a_copies + [fwd_right, fwd_left]:
        copy.wait_send()
    drain(rbuf.at[pl.ds(0, 6)], am_send)
    drain(cown.at[pl.ds(0, 28)], c2_send)

    @pl.when(own_target)
    def _():
        drain(cown.at[pl.ds(0, RING - 1)], c1_send)

    drain(lbuf.at[pl.ds(0, HALF - 1)], b_send)
    drain(sbuf.at[pl.ds(0, HALF - 1)], e_send)

    @pl.when(jnp.logical_not(own_target))
    def _():
        drain(lbuf.at[0], b_send)
        drain(sbuf.at[0], e_send)

    drain(lbuf.at[pl.ds(0, HALF)], bm_send)
    drain(fbuf.at[pl.ds(0, HALF)], f_send)


def body(weather, response, coupling, sources, delays):
    rows_of_lags = response.reshape(BS * GROUP, CH)
    bf16, f32 = jnp.bfloat16, jnp.float32
    vm, dma = pltpu.VMEM, pltpu.SemaphoreType.DMA
    rows = pl.pallas_call(
        kernel,
        out_shape=jax.ShapeDtypeStruct((QUARTER, BS), bf16),
        in_specs=[pl.BlockSpec(memory_space=pltpu.HBM)] * 3
        + [pl.BlockSpec(memory_space=pltpu.SMEM)] * 2,
        out_specs=pl.BlockSpec(memory_space=pl.ANY),
        scratch_shapes=[
            vm((BS * GROUP, CH), bf16),
            vm((BS * GROUP, CH), f32),
            vm((WPRE + QUARTER, CH), bf16),
            vm((WPRE + QUARTER, CH), f32),
            vm((XROWS, GROUP * CH), bf16),
            vm((16, BS, PIECE * CH), bf16),
            vm((EXT, BS), f32),
            vm((EXT, BS), bf16),
            vm((BLOCKS, LROWS, BS), bf16),
            vm((BLOCKS, LROWS, BS), f32),
            vm((BLOCKS, FROWS, BS), bf16),
            vm((BLOCKS, FROWS, BS), f32),
            vm((HALF, ROWS, BS), bf16),
            vm((HALF, 2, BS, BS), bf16),
            dma((2,)),
            dma,
            dma((6,)),
            dma((6,)),
            dma,
            dma((3,)),
            dma,
            dma((4,)),
            dma,
            dma((32,)),
            dma,
            dma((4,)),
            dma,
            dma((4,)),
            dma,
            dma((4,)),
            dma,
            dma,
        ],
        compiler_params=pltpu.CompilerParams(
            collective_id=0, has_side_effects=True, vmem_limit_bytes=60 * 1024 * 1024
        ),
    )(weather, rows_of_lags, coupling, sources.T, delays.T)
    return rows.T


def solution(mesh):
    placed = (P("scen", None), P("wide", "blk", None), P("wide", None, None, None), P(), P())
    return jax.shard_map(
        body, mesh=mesh, in_specs=placed, out_specs=P(("scen", "wide"), "blk"), check_vma=False
    )
```

```python
import functools

import jax
import jax.numpy as jnp
from jax import lax
from jax.experimental import pallas as pl
from jax.experimental.pallas import tpu as pltpu
from jax.sharding import PartitionSpec as P

MESH = pl.DeviceIdType.MESH
CH = 128
LAGS = 64
BS = 128
HALO = 16
RING = 8
BLOCKS = 64
HALF = 32
ROWS = 32
QUARTER = HALF * ROWS
EXT = QUARTER + 2 * HALO
LROWS = ROWS + 2 * HALO
FROWS = ROWS + HALO
PIECE = 4
PARTS = 4
GROUP = 16
XROWS = EXT + LAGS - GROUP
WPRE = 96
TILE = 352
STRIDE = 5


def drain(ref, sem):
    pltpu.make_async_copy(ref, ref, sem).wait()


def kernel(
    weather,
    resp,
    coupling,
    sources,
    delays,
    out,
    rraw,
    r32,
    wraw,
    w32,
    xbuf,
    rbuf,
    acc,
    lext,
    lbuf,
    l32,
    fbuf,
    f32b,
    sbuf,
    cown,
    loc_sem,
    own_sem,
    a_send,
    a_recv,
    am_send,
    am_recv,
    c1_send,
    c1_recv,
    c2_send,
    c2_recv,
    b_send,
    b_recv,
    bm_send,
    bm_recv,
    f_send,
    f_recv,
    e_send,
    e_recv,
):
    s = lax.axis_index("scen")
    w = lax.axis_index("wide")
    x = lax.axis_index("blk")
    y, z = w // RING, w % RING
    first_core = s == 0
    u = jnp.where(first_core, z, y)
    v = jnp.where(first_core, y, z)
    right, left = (x + 1) % PARTS, (x + PARTS - 1) % PARTS
    far = (x + 2) % PARTS

    def wide_of(uu, vv):
        return jnp.where(first_core, vv * RING + uu, uu * RING + vv)

    def remote(src, dst, send, recv, core, wide, blk):
        return pltpu.make_async_remote_copy(
            src_ref=src,
            dst_ref=dst,
            send_sem=send,
            recv_sem=recv,
            device_id=(core, wide, blk),
            device_id_type=MESH,
        )

    sister = (1 - s, w, x)
    core_t = (y + z) % 2
    slot = w // 2

    def chip(core, m):
        return 2 * m + (core + m // 4) % 2

    own_target = core_t == s

    lead = pl.multiple_of(jnp.maximum(x * QUARTER - WPRE, 0), 32)
    here = pl.multiple_of(x * QUARTER, QUARTER)
    main_copy = pltpu.make_async_copy(
        weather.at[pl.ds(here, QUARTER)], wraw.at[pl.ds(WPRE, QUARTER)], loc_sem.at[0]
    )
    lead_copy = pltpu.make_async_copy(
        weather.at[pl.ds(lead, WPRE)], wraw.at[pl.ds(0, WPRE)], loc_sem.at[1]
    )
    resp_copy = pltpu.make_async_copy(resp, rraw, own_sem)
    resp_copy.start()
    main_copy.start()
    lead_copy.start()

    barrier = pltpu.get_barrier_semaphore()

    def greet(core, wide, blk):
        pl.semaphore_signal(barrier, inc=1, device_id=(core, wide, blk), device_id_type=MESH)

    greet(s, w, right)
    greet(s, w, left)
    greet(*sister)

    @pl.loop(1, RING)
    def _(step):
        greet(s, wide_of((u + step) % RING, v), x)

    greet(s, wide_of(u, (v + 1) % RING), x)
    greet(s, wide_of(u, (v + RING - 1) % RING), x)

    @pl.loop(1, HALF)
    def _(step):
        greet(core_t, chip(s, (slot + step) % HALF), x)

    @pl.when(jnp.logical_not(own_target))
    def _():
        greet(core_t, chip(s, slot), x)

    def lay_out(core):
        for lag in range(GROUP // 2):
            column = (lag % PIECE) * CH
            rbuf[4 * x + 2 * core + lag // PIECE, :, column : column + CH] = r32[
                pl.ds(GROUP // 2 * core + lag, BS, stride=GROUP), :
            ].astype(jnp.bfloat16)

    resp_copy.wait()
    r32[...] = rraw[...].astype(jnp.float32)
    lay_out(s)

    pl.semaphore_wait(barrier, 3 + RING - 1 + 2 + HALF - 1 + jnp.where(own_target, 0, 1))

    def a_copy(index, src, piece, blk):
        return remote(src, rbuf.at[piece], a_send.at[index], a_recv.at[index], s, w, blk)

    p0, p1 = 2 * s, 2 * s + 1
    a_copies = [
        a_copy(0, rbuf.at[4 * x + p0], 4 * x + p0, right),
        a_copy(1, rbuf.at[4 * x + p1], 4 * x + p1, left),
        a_copy(2, rbuf.at[4 * x + p1], 4 * x + p1, right),
        a_copy(3, rbuf.at[4 * x + p0], 4 * x + p0, left),
    ]
    for copy in a_copies:
        copy.start()

    @pl.when(own_target)
    def _():
        pltpu.make_async_copy(coupling.at[0], cown.at[4 * v], c1_recv.at[0]).start()
        for away, place in ((1, 1), (7, 0), (2, 2), (6, 1), (3, 3), (5, 2), (4, 3)):
            remote(
                coupling.at[0],
                cown.at[4 * v + place],
                c1_send,
                c1_recv.at[place],
                s,
                wide_of((u + away) % RING, v),
                x,
            ).start()

    def c_step(way, step, piece):
        if way == 0:
            row, to = (v + RING - step + 1) % RING, (v + 1) % RING
        else:
            row, to = (v + step - 1) % RING, (v + RING - 1) % RING
        part = cown.at[4 * row + piece]
        index = (way * 4 + step - 1) * 4 + piece
        return remote(part, part, c2_send, c2_recv.at[index], s, wide_of(u, to), x)

    def goes(way, step, piece):
        return step < 4 or (step == 4 and piece // 2 == way)

    def c_begin(*pieces):
        for piece in pieces:
            drain(cown.at[0], c1_recv.at[piece])
            for way in range(2):
                c_step(way, 1, piece).start()

    def c_arrive(step, *pieces):
        for piece in pieces:
            for way in range(2):
                if goes(way, step, piece):
                    c_step(way, step, piece).wait_recv()
                    if goes(way, step + 1, piece):
                        c_step(way, step + 1, piece).start()

    main_copy.wait()
    lead_copy.wait()

    @pl.when(x == 0)
    def _():
        wraw[pl.ds(0, WPRE), :] = jnp.zeros((WPRE, CH), jnp.bfloat16)

    w32[...] = wraw[...].astype(jnp.float32)

    def columns(first, last):
        for lag in range(first, last):
            xbuf[:, lag * CH : (lag + 1) * CH] = w32[GROUP - lag : GROUP - lag + XROWS, :].astype(
                jnp.bfloat16
            )

    columns(0, 8)
    c_begin(0)
    columns(8, 16)
    c_begin(1)

    def add_groups(groups, tile, first=False):
        total = None if first else acc[pl.ds(tile * TILE, TILE), :]
        for group in groups:
            start = pl.multiple_of((LAGS - GROUP) - GROUP * group + tile * TILE, 16)
            for piece in range(4):
                term = lax.dot_general(
                    xbuf[pl.ds(start, TILE), piece * PIECE * CH : (piece + 1) * PIECE * CH],
                    rbuf[4 * group + piece],
                    (((1,), (1,)), ((), ())),
                    preferred_element_type=jnp.float32,
                )
                total = term if total is None else total + term
        return total

    def add_far(core, tile):
        start = pl.multiple_of((LAGS - GROUP) - GROUP * far + tile * TILE, 16)
        total = acc[pl.ds(tile * TILE, TILE), :]
        for half in range(2):
            piece = 2 * core + half
            column = pl.multiple_of(piece * PIECE * CH, PIECE * CH)
            total = total + lax.dot_general(
                xbuf[pl.ds(start, TILE), pl.ds(column, PIECE * CH)],
                rbuf[4 * far + piece],
                (((1,), (1,)), ((), ())),
                preferred_element_type=jnp.float32,
            )
        return total

    def keep(tile, total):
        acc[pl.ds(tile * TILE, TILE), :] = total

    lay_out(1 - s)
    keep(0, add_groups([x], 0, True))
    keep(1, add_groups([x], 1, True))

    def mirror_piece(piece, group_sem):
        remote(
            rbuf.at[piece], rbuf.at[piece], am_send, am_recv.at[group_sem], *sister
        ).start()

    a_copies[0].wait_recv()
    fwd_right = a_copy(4, rbuf.at[4 * left + p0], 4 * left + p0, right)
    fwd_right.start()
    a_copies[1].wait_recv()
    fwd_left = a_copy(5, rbuf.at[4 * right + p1], 4 * right + p1, left)
    fwd_left.start()
    mirror_piece(4 * left + p0, 0)
    mirror_piece(4 * right + p1, 1)

    c_begin(2)
    c_arrive(1, 0)
    keep(2, add_groups([x], 2, True))
    c_begin(3)
    c_arrive(1, 1)
    a_copies[2].wait_recv()
    mirror_piece(4 * left + p1, 0)
    a_copies[3].wait_recv()
    mirror_piece(4 * right + p0, 1)
    c_arrive(1, 2, 3)
    c_arrive(2, 0)
    drain(rbuf.at[pl.ds(0, 2)], am_recv.at[0])
    drain(rbuf.at[pl.ds(0, 2)], am_recv.at[1])
    keep(0, add_groups([left, right], 0))
    c_arrive(2, 1)
    keep(1, add_groups([left, right], 1))
    c_arrive(2, 2)
    fwd_right.wait_recv()
    mirror_piece(4 * far + p0, 2)
    fwd_left.wait_recv()
    mirror_piece(4 * far + p1, 2)
    keep(2, add_groups([left, right], 2))
    for tile in range(3):
        keep(tile, add_far(s, tile))
    c_arrive(2, 3)
    drain(rbuf.at[pl.ds(0, 2)], am_recv.at[2])
    for tile in range(3):
        lext[pl.ds(tile * TILE, TILE), :] = add_far(1 - s, tile).astype(jnp.bfloat16)

    def b_copy(step):
        i = (slot + STRIDE * step) % HALF
        return remote(
            lext.at[pl.ds(pl.multiple_of(ROWS * i, ROWS), LROWS)],
            lbuf.at[HALF * core_t + slot],
            b_send,
            b_recv.at[slot // 8],
            core_t,
            chip(s, i),
            x,
        )

    @pl.when(own_target)
    def _():
        pltpu.make_async_copy(
            lext.at[pl.ds(pl.multiple_of(ROWS * slot, ROWS), LROWS)],
            lbuf.at[HALF * core_t + slot],
            b_recv.at[slot // 8],
        ).start()

    @pl.when(jnp.logical_not(own_target))
    def _():
        b_copy(0).start()

    @pl.loop(1, HALF)
    def _(step):
        b_copy(step).start()

    c_arrive(3, 0, 1, 2, 3)
    c_arrive(4, 0, 2, 1, 3)

    mine = HALF * s
    theirs = HALF * (1 - s)

    def mirror(buf, first, count, send, recv):
        part = buf.at[pl.ds(first, count)]
        return remote(part, part, send, recv, *sister)

    def widen(first):
        l32[pl.ds(first, 8)] = lbuf[pl.ds(first, 8)].astype(jnp.float32)

    for part in range(4):
        drain(lbuf.at[pl.ds(0, 8)], b_recv.at[part])
        mirror(lbuf, mine + 8 * part, 8, bm_send, bm_recv.at[part]).start()
    for part in range(4):
        widen(mine + 8 * part)
    for part in range(4):
        drain(lbuf.at[pl.ds(0, 8)], bm_recv.at[part])
        widen(theirs + 8 * part)

    def block_of(wide):
        return HALF * ((wide // RING + wide) % 2) + wide // 2

    def moved(series, m, start, rows):
        wide = chip(s, m)
        upstream = [
            series[block_of(sources[k, wide]), pl.ds(start - delays[k, wide], rows), :]
            for k in range(2)
        ]
        lhs = jnp.concatenate(upstream, axis=1).astype(jnp.bfloat16)
        wy, wz = wide // RING, wide % RING
        row = jnp.where(first_core, wy, wz)
        away = (jnp.where(first_core, wz, wy) - u + RING) % RING
        place = jnp.where(
            away % 2 == 0,
            jnp.where(away == 0, 0, jnp.where(away == 2, 1, jnp.where(away == 6, 2, 3))),
            jnp.where(away == 1, 0, jnp.where(away == 7, 1, jnp.where(away == 3, 2, 3))),
        )
        rhs = cown[4 * row + place].reshape(2 * BS, BS)
        return jnp.dot(lhs, rhs, preferred_element_type=jnp.float32)

    for part in range(4):

        @pl.loop(0, 8, unroll=8)
        def _(m):
            i = mine + 8 * part + m
            total = l32[i, HALO:LROWS, :] + moved(l32, 8 * part + m, HALO, FROWS)
            rounded = total.astype(jnp.bfloat16)
            fbuf[i] = rounded
            f32b[i] = rounded.astype(jnp.float32)

        mirror(fbuf, mine + 8 * part, 8, f_send, f_recv.at[part]).start()

    for part in range(4):
        drain(fbuf.at[pl.ds(0, 8)], f_recv.at[part])
        f32b[pl.ds(theirs + 8 * part, 8)] = fbuf[pl.ds(theirs + 8 * part, 8)].astype(jnp.float32)

    span = pl.ds(pl.multiple_of(ROWS * slot, ROWS), ROWS)

    def second(m):
        i = mine + m
        total = f32b[i, HALO:FROWS, :] + moved(f32b, m, HALO, ROWS)
        sbuf[m] = total.astype(jnp.bfloat16)

    def e_copy(m):
        return remote(sbuf.at[m], out.at[span], e_send, e_recv, core_t, chip(s, m), x)

    def e_local():
        return pltpu.make_async_copy(sbuf.at[slot], out.at[span], e_recv)

    @pl.loop(0, 4)
    def _(column):
        for start in (0, 4):
            picked = [4 * ((y + start + k) % RING) + column for k in range(4)]
            for m in picked:
                second(m)
            for k, m in enumerate(picked):
                if start + k > 0:
                    e_copy(m).start()
                    continue
                stays = jnp.logical_and(own_target, m == slot)

                @pl.when(stays)
                def _():
                    e_local().start()

                @pl.when(jnp.logical_not(stays))
                def _():
                    e_copy(m).start()

    drain(out, e_recv)
    for copy in a_copies + [fwd_right, fwd_left]:
        copy.wait_send()
    drain(rbuf.at[pl.ds(0, 6)], am_send)
    drain(cown.at[pl.ds(0, 28)], c2_send)

    @pl.when(own_target)
    def _():
        drain(cown.at[pl.ds(0, RING - 1)], c1_send)

    drain(lbuf.at[pl.ds(0, HALF - 1)], b_send)
    drain(sbuf.at[pl.ds(0, HALF - 1)], e_send)

    @pl.when(jnp.logical_not(own_target))
    def _():
        drain(lbuf.at[0], b_send)
        drain(sbuf.at[0], e_send)

    drain(lbuf.at[pl.ds(0, HALF)], bm_send)
    drain(fbuf.at[pl.ds(0, HALF)], f_send)


def body(weather, response, coupling, sources, delays):
    rows_of_lags = response.reshape(BS * GROUP, CH)
    bf16, f32 = jnp.bfloat16, jnp.float32
    vm, dma = pltpu.VMEM, pltpu.SemaphoreType.DMA
    rows = pl.pallas_call(
        kernel,
        out_shape=jax.ShapeDtypeStruct((QUARTER, BS), bf16),
        in_specs=[pl.BlockSpec(memory_space=pltpu.HBM)] * 3
        + [pl.BlockSpec(memory_space=pltpu.SMEM)] * 2,
        out_specs=pl.BlockSpec(memory_space=pl.ANY),
        scratch_shapes=[
            vm((BS * GROUP, CH), bf16),
            vm((BS * GROUP, CH), f32),
            vm((WPRE + QUARTER, CH), bf16),
            vm((WPRE + QUARTER, CH), f32),
            vm((XROWS, GROUP * CH), bf16),
            vm((16, BS, PIECE * CH), bf16),
            vm((EXT, BS), f32),
            vm((EXT, BS), bf16),
            vm((BLOCKS, LROWS, BS), bf16),
            vm((BLOCKS, LROWS, BS), f32),
            vm((BLOCKS, FROWS, BS), bf16),
            vm((BLOCKS, FROWS, BS), f32),
            vm((HALF, ROWS, BS), bf16),
            vm((HALF, 2, BS, BS), bf16),
            dma((2,)),
            dma,
            dma((6,)),
            dma((6,)),
            dma,
            dma((3,)),
            dma,
            dma((4,)),
            dma,
            dma((32,)),
            dma,
            dma((4,)),
            dma,
            dma((4,)),
            dma,
            dma((4,)),
            dma,
            dma,
        ],
        compiler_params=pltpu.CompilerParams(
            collective_id=0, has_side_effects=True, vmem_limit_bytes=60 * 1024 * 1024
        ),
    )(weather, rows_of_lags, coupling, sources.T, delays.T)
    return rows.T


def solution(mesh):
    placed = (P("scen", None), P("wide", "blk", None), P("wide", None, None, None), P(), P())
    return jax.shard_map(
        body, mesh=mesh, in_specs=placed, out_specs=P(("scen", "wide"), "blk"), check_vma=False
    )
```

```python
import functools

import jax
import jax.numpy as jnp
from jax import lax
from jax.experimental import pallas as pl
from jax.experimental.pallas import tpu as pltpu
from jax.sharding import PartitionSpec as P

MESH = pl.DeviceIdType.MESH
CH = 128
LAGS = 64
BS = 128
HALO = 16
RING = 8
BLOCKS = 64
HALF = 32
ROWS = 32
QUARTER = HALF * ROWS
EXT = QUARTER + 2 * HALO
LROWS = ROWS + 2 * HALO
FROWS = ROWS + HALO
PIECE = 4
PARTS = 4
GROUP = 16
XROWS = EXT + LAGS - GROUP
WPRE = 96
TILE = 352
STRIDE = 5


def drain(ref, sem):
    pltpu.make_async_copy(ref, ref, sem).wait()


def kernel(
    weather,
    resp,
    coupling,
    sources,
    delays,
    out,
    rraw,
    r32,
    wraw,
    w32,
    xbuf,
    rbuf,
    acc,
    lext,
    lbuf,
    l32,
    fbuf,
    f32b,
    sbuf,
    cown,
    loc_sem,
    own_sem,
    a_send,
    a_recv,
    am_send,
    am_recv,
    c1_send,
    c1_recv,
    c2_send,
    c2_recv,
    b_send,
    b_recv,
    bm_send,
    bm_recv,
    f_send,
    f_recv,
    e_send,
    e_recv,
):
    s = lax.axis_index("scen")
    w = lax.axis_index("wide")
    x = lax.axis_index("blk")
    y, z = w // RING, w % RING
    first_core = s == 0
    u = jnp.where(first_core, z, y)
    v = jnp.where(first_core, y, z)
    right, left = (x + 1) % PARTS, (x + PARTS - 1) % PARTS
    far = (x + 2) % PARTS

    def wide_of(uu, vv):
        return jnp.where(first_core, vv * RING + uu, uu * RING + vv)

    def remote(src, dst, send, recv, core, wide, blk):
        return pltpu.make_async_remote_copy(
            src_ref=src,
            dst_ref=dst,
            send_sem=send,
            recv_sem=recv,
            device_id=(core, wide, blk),
            device_id_type=MESH,
        )

    sister = (1 - s, w, x)
    core_t = (y + z) % 2
    slot = w // 2

    def chip(core, m):
        return 2 * m + (core + m // 4) % 2

    own_target = core_t == s

    lead = pl.multiple_of(jnp.maximum(x * QUARTER - WPRE, 0), 32)
    here = pl.multiple_of(x * QUARTER, QUARTER)
    main_copy = pltpu.make_async_copy(
        weather.at[pl.ds(here, QUARTER)], wraw.at[pl.ds(WPRE, QUARTER)], loc_sem.at[0]
    )
    lead_copy = pltpu.make_async_copy(
        weather.at[pl.ds(lead, WPRE)], wraw.at[pl.ds(0, WPRE)], loc_sem.at[1]
    )
    resp_copy = pltpu.make_async_copy(resp, rraw, own_sem)
    resp_copy.start()
    main_copy.start()
    lead_copy.start()

    barrier = pltpu.get_barrier_semaphore()

    def greet(core, wide, blk):
        pl.semaphore_signal(barrier, inc=1, device_id=(core, wide, blk), device_id_type=MESH)

    greet(s, w, right)
    greet(s, w, left)
    greet(*sister)

    @pl.loop(1, RING)
    def _(step):
        greet(s, wide_of((u + step) % RING, v), x)

    greet(s, wide_of(u, (v + 1) % RING), x)
    greet(s, wide_of(u, (v + RING - 1) % RING), x)

    @pl.loop(1, HALF)
    def _(step):
        greet(core_t, chip(s, (slot + step) % HALF), x)

    @pl.when(jnp.logical_not(own_target))
    def _():
        greet(core_t, chip(s, slot), x)

    def lay_out(core):
        for lag in range(GROUP // 2):
            column = (lag % PIECE) * CH
            rbuf[4 * x + 2 * core + lag // PIECE, :, column : column + CH] = r32[
                pl.ds(GROUP // 2 * core + lag, BS, stride=GROUP), :
            ].astype(jnp.bfloat16)

    resp_copy.wait()
    r32[...] = rraw[...].astype(jnp.float32)
    lay_out(s)

    pl.semaphore_wait(barrier, 3 + RING - 1 + 2 + HALF - 1 + jnp.where(own_target, 0, 1))

    def a_copy(index, src, piece, blk):
        return remote(src, rbuf.at[piece], a_send.at[index], a_recv.at[index], s, w, blk)

    p0, p1 = 2 * s, 2 * s + 1
    a_copies = [
        a_copy(0, rbuf.at[4 * x + p0], 4 * x + p0, right),
        a_copy(1, rbuf.at[4 * x + p1], 4 * x + p1, left),
        a_copy(2, rbuf.at[4 * x + p1], 4 * x + p1, right),
        a_copy(3, rbuf.at[4 * x + p0], 4 * x + p0, left),
    ]
    for copy in a_copies:
        copy.start()

    @pl.when(own_target)
    def _():
        pltpu.make_async_copy(coupling.at[0], cown.at[4 * v], c1_recv.at[0]).start()
        for away, place in ((1, 1), (7, 0), (2, 2), (6, 1), (3, 3), (5, 2), (4, 3)):
            remote(
                coupling.at[0],
                cown.at[4 * v + place],
                c1_send,
                c1_recv.at[place],
                s,
                wide_of((u + away) % RING, v),
                x,
            ).start()

    def c_step(way, step, piece):
        if way == 0:
            row, to = (v + RING - step + 1) % RING, (v + 1) % RING
        else:
            row, to = (v + step - 1) % RING, (v + RING - 1) % RING
        part = cown.at[4 * row + piece]
        index = (way * 4 + step - 1) * 4 + piece
        return remote(part, part, c2_send, c2_recv.at[index], s, wide_of(u, to), x)

    def goes(way, step, piece):
        return step < 4 or (step == 4 and piece // 2 == way)

    def c_begin(*pieces):
        for piece in pieces:
            drain(cown.at[0], c1_recv.at[piece])
            for way in range(2):
                c_step(way, 1, piece).start()

    def c_arrive(step, *pieces):
        for piece in pieces:
            for way in range(2):
                if goes(way, step, piece):
                    c_step(way, step, piece).wait_recv()
                    if goes(way, step + 1, piece):
                        c_step(way, step + 1, piece).start()

    main_copy.wait()
    lead_copy.wait()

    @pl.when(x == 0)
    def _():
        wraw[pl.ds(0, WPRE), :] = jnp.zeros((WPRE, CH), jnp.bfloat16)

    w32[...] = wraw[...].astype(jnp.float32)

    def columns(first, last):
        for lag in range(first, last):
            xbuf[:, lag * CH : (lag + 1) * CH] = w32[GROUP - lag : GROUP - lag + XROWS, :].astype(
                jnp.bfloat16
            )

    columns(0, 8)
    c_begin(0)
    columns(8, 16)
    c_begin(1)

    def add_groups(groups, tile, first=False):
        total = None if first else acc[pl.ds(tile * TILE, TILE), :]
        for group in groups:
            start = pl.multiple_of((LAGS - GROUP) - GROUP * group + tile * TILE, 16)
            for piece in range(4):
                term = lax.dot_general(
                    xbuf[pl.ds(start, TILE), piece * PIECE * CH : (piece + 1) * PIECE * CH],
                    rbuf[4 * group + piece],
                    (((1,), (1,)), ((), ())),
                    preferred_element_type=jnp.float32,
                )
                total = term if total is None else total + term
        return total

    def add_far(core, tile):
        start = pl.multiple_of((LAGS - GROUP) - GROUP * far + tile * TILE, 16)
        total = acc[pl.ds(tile * TILE, TILE), :]
        for half in range(2):
            piece = 2 * core + half
            column = pl.multiple_of(piece * PIECE * CH, PIECE * CH)
            total = total + lax.dot_general(
                xbuf[pl.ds(start, TILE), pl.ds(column, PIECE * CH)],
                rbuf[4 * far + piece],
                (((1,), (1,)), ((), ())),
                preferred_element_type=jnp.float32,
            )
        return total

    def keep(tile, total):
        acc[pl.ds(tile * TILE, TILE), :] = total

    lay_out(1 - s)
    keep(0, add_groups([x], 0, True))
    keep(1, add_groups([x], 1, True))

    def mirror_piece(piece, group_sem):
        remote(
            rbuf.at[piece], rbuf.at[piece], am_send, am_recv.at[group_sem], *sister
        ).start()

    a_copies[0].wait_recv()
    fwd_right = a_copy(4, rbuf.at[4 * left + p0], 4 * left + p0, right)
    fwd_right.start()
    a_copies[1].wait_recv()
    fwd_left = a_copy(5, rbuf.at[4 * right + p1], 4 * right + p1, left)
    fwd_left.start()
    mirror_piece(4 * left + p0, 0)
    mirror_piece(4 * right + p1, 1)

    c_begin(2)
    c_arrive(1, 0)
    keep(2, add_groups([x], 2, True))
    c_begin(3)
    c_arrive(1, 1)
    a_copies[2].wait_recv()
    mirror_piece(4 * left + p1, 0)
    a_copies[3].wait_recv()
    mirror_piece(4 * right + p0, 1)
    c_arrive(1, 2, 3)
    c_arrive(2, 0)
    drain(rbuf.at[pl.ds(0, 2)], am_recv.at[0])
    drain(rbuf.at[pl.ds(0, 2)], am_recv.at[1])
    keep(0, add_groups([left, right], 0))
    c_arrive(2, 1)
    keep(1, add_groups([left, right], 1))
    c_arrive(2, 2)
    fwd_right.wait_recv()
    mirror_piece(4 * far + p0, 2)
    fwd_left.wait_recv()
    mirror_piece(4 * far + p1, 2)
    keep(2, add_groups([left, right], 2))
    for tile in range(3):
        keep(tile, add_far(s, tile))
    c_arrive(2, 3)
    drain(rbuf.at[pl.ds(0, 2)], am_recv.at[2])
    for tile in range(3):
        lext[pl.ds(tile * TILE, TILE), :] = add_far(1 - s, tile).astype(jnp.bfloat16)

    def b_copy(step):
        i = (slot + STRIDE * step) % HALF
        return remote(
            lext.at[pl.ds(pl.multiple_of(ROWS * i, ROWS), LROWS)],
            lbuf.at[HALF * core_t + slot],
            b_send,
            b_recv.at[slot // 8],
            core_t,
            chip(s, i),
            x,
        )

    @pl.when(own_target)
    def _():
        pltpu.make_async_copy(
            lext.at[pl.ds(pl.multiple_of(ROWS * slot, ROWS), LROWS)],
            lbuf.at[HALF * core_t + slot],
            b_recv.at[slot // 8],
        ).start()

    @pl.when(jnp.logical_not(own_target))
    def _():
        b_copy(0).start()

    @pl.loop(1, HALF)
    def _(step):
        b_copy(step).start()

    c_arrive(3, 0, 1, 2, 3)
    c_arrive(4, 0, 2, 1, 3)

    mine = HALF * s
    theirs = HALF * (1 - s)

    def mirror(buf, first, count, send, recv):
        part = buf.at[pl.ds(first, count)]
        return remote(part, part, send, recv, *sister)

    def widen(first):
        l32[pl.ds(first, 8)] = lbuf[pl.ds(first, 8)].astype(jnp.float32)

    for part in range(4):
        drain(lbuf.at[pl.ds(0, 8)], b_recv.at[part])
        mirror(lbuf, mine + 8 * part, 8, bm_send, bm_recv.at[part]).start()
    for part in range(4):
        widen(mine + 8 * part)
    for part in range(4):
        drain(lbuf.at[pl.ds(0, 8)], bm_recv.at[part])
        widen(theirs + 8 * part)

    def block_of(wide):
        return HALF * ((wide // RING + wide) % 2) + wide // 2

    def moved(series, m, start, rows):
        wide = chip(s, m)
        upstream = [
            series[block_of(sources[k, wide]), pl.ds(start - delays[k, wide], rows), :]
            for k in range(2)
        ]
        lhs = jnp.concatenate(upstream, axis=1).astype(jnp.bfloat16)
        wy, wz = wide // RING, wide % RING
        row = jnp.where(first_core, wy, wz)
        away = (jnp.where(first_core, wz, wy) - u + RING) % RING
        place = jnp.where(
            away % 2 == 0,
            jnp.where(away == 0, 0, jnp.where(away == 2, 1, jnp.where(away == 6, 2, 3))),
            jnp.where(away == 1, 0, jnp.where(away == 7, 1, jnp.where(away == 3, 2, 3))),
        )
        rhs = cown[4 * row + place].reshape(2 * BS, BS)
        return jnp.dot(lhs, rhs, preferred_element_type=jnp.float32)

    for part in range(4):

        @pl.loop(0, 8, unroll=8)
        def _(m):
            i = mine + 8 * part + m
            total = l32[i, HALO:LROWS, :] + moved(l32, 8 * part + m, HALO, FROWS)
            rounded = total.astype(jnp.bfloat16)
            fbuf[i] = rounded
            f32b[i] = rounded.astype(jnp.float32)

        mirror(fbuf, mine + 8 * part, 8, f_send, f_recv.at[part]).start()

    for part in range(4):
        drain(fbuf.at[pl.ds(0, 8)], f_recv.at[part])
        f32b[pl.ds(theirs + 8 * part, 8)] = fbuf[pl.ds(theirs + 8 * part, 8)].astype(jnp.float32)

    span = pl.ds(pl.multiple_of(ROWS * slot, ROWS), ROWS)

    def second(m):
        i = mine + m
        total = f32b[i, HALO:FROWS, :] + moved(f32b, m, HALO, ROWS)
        sbuf[m] = total.astype(jnp.bfloat16)

    def e_copy(m):
        return remote(sbuf.at[m], out.at[span], e_send, e_recv, core_t, chip(s, m), x)

    def e_local():
        return pltpu.make_async_copy(sbuf.at[slot], out.at[span], e_recv)

    @pl.loop(0, 4)
    def _(column):
        for row in (s, 1 - s):
            picked = [4 * (row + 2 * ((y // 2 + k) % 4)) + column for k in range(4)]
            for m in picked:
                second(m)
            for k, m in enumerate(picked):
                if k > 0:
                    e_copy(m).start()
                    continue
                stays = jnp.logical_and(own_target, m == slot)

                @pl.when(stays)
                def _():
                    e_local().start()

                @pl.when(jnp.logical_not(stays))
                def _():
                    e_copy(m).start()

    drain(out, e_recv)
    for copy in a_copies + [fwd_right, fwd_left]:
        copy.wait_send()
    drain(rbuf.at[pl.ds(0, 6)], am_send)
    drain(cown.at[pl.ds(0, 28)], c2_send)

    @pl.when(own_target)
    def _():
        drain(cown.at[pl.ds(0, RING - 1)], c1_send)

    drain(lbuf.at[pl.ds(0, HALF - 1)], b_send)
    drain(sbuf.at[pl.ds(0, HALF - 1)], e_send)

    @pl.when(jnp.logical_not(own_target))
    def _():
        drain(lbuf.at[0], b_send)
        drain(sbuf.at[0], e_send)

    drain(lbuf.at[pl.ds(0, HALF)], bm_send)
    drain(fbuf.at[pl.ds(0, HALF)], f_send)


def body(weather, response, coupling, sources, delays):
    rows_of_lags = response.reshape(BS * GROUP, CH)
    bf16, f32 = jnp.bfloat16, jnp.float32
    vm, dma = pltpu.VMEM, pltpu.SemaphoreType.DMA
    rows = pl.pallas_call(
        kernel,
        out_shape=jax.ShapeDtypeStruct((QUARTER, BS), bf16),
        in_specs=[pl.BlockSpec(memory_space=pltpu.HBM)] * 3
        + [pl.BlockSpec(memory_space=pltpu.SMEM)] * 2,
        out_specs=pl.BlockSpec(memory_space=pl.ANY),
        scratch_shapes=[
            vm((BS * GROUP, CH), bf16),
            vm((BS * GROUP, CH), f32),
            vm((WPRE + QUARTER, CH), bf16),
            vm((WPRE + QUARTER, CH), f32),
            vm((XROWS, GROUP * CH), bf16),
            vm((16, BS, PIECE * CH), bf16),
            vm((EXT, BS), f32),
            vm((EXT, BS), bf16),
            vm((BLOCKS, LROWS, BS), bf16),
            vm((BLOCKS, LROWS, BS), f32),
            vm((BLOCKS, FROWS, BS), bf16),
            vm((BLOCKS, FROWS, BS), f32),
            vm((HALF, ROWS, BS), bf16),
            vm((HALF, 2, BS, BS), bf16),
            dma((2,)),
            dma,
            dma((6,)),
            dma((6,)),
            dma,
            dma((3,)),
            dma,
            dma((4,)),
            dma,
            dma((32,)),
            dma,
            dma((4,)),
            dma,
            dma((4,)),
            dma,
            dma((4,)),
            dma,
            dma,
        ],
        compiler_params=pltpu.CompilerParams(
            collective_id=0, has_side_effects=True, vmem_limit_bytes=60 * 1024 * 1024
        ),
    )(weather, rows_of_lags, coupling, sources.T, delays.T)
    return rows.T


def solution(mesh):
    placed = (P("scen", None), P("wide", "blk", None), P("wide", None, None, None), P(), P())
    return jax.shard_map(
        body, mesh=mesh, in_specs=placed, out_specs=P(("scen", "wide"), "blk"), check_vma=False
    )
```

```python
import functools

import jax
import jax.numpy as jnp
from jax import lax
from jax.experimental import pallas as pl
from jax.experimental.pallas import tpu as pltpu
from jax.sharding import PartitionSpec as P

MESH = pl.DeviceIdType.MESH
CH = 128
LAGS = 64
BS = 128
HALO = 16
RING = 8
BLOCKS = 64
HALF = 32
ROWS = 32
QUARTER = HALF * ROWS
EXT = QUARTER + 2 * HALO
LROWS = ROWS + 2 * HALO
FROWS = ROWS + HALO
PIECE = 4
PARTS = 4
GROUP = 16
XROWS = EXT + LAGS - GROUP
WPRE = 96
TILE = 352
STRIDE = 5


def drain(ref, sem):
    pltpu.make_async_copy(ref, ref, sem).wait()


def kernel(
    weather,
    resp,
    coupling,
    sources,
    delays,
    out,
    rraw,
    r32,
    wraw,
    w32,
    xbuf,
    rbuf,
    acc,
    lext,
    lbuf,
    l32,
    fbuf,
    f32b,
    sbuf,
    cown,
    loc_sem,
    own_sem,
    a_send,
    a_recv,
    am_send,
    am_recv,
    c1_send,
    c1_recv,
    c2_send,
    c2_recv,
    b_send,
    b_recv,
    bm_send,
    bm_recv,
    f_send,
    f_recv,
    e_send,
    e_recv,
):
    s = lax.axis_index("scen")
    w = lax.axis_index("wide")
    x = lax.axis_index("blk")
    y, z = w // RING, w % RING
    first_core = s == 0
    u = jnp.where(first_core, z, y)
    v = jnp.where(first_core, y, z)
    right, left = (x + 1) % PARTS, (x + PARTS - 1) % PARTS
    far = (x + 2) % PARTS

    def wide_of(uu, vv):
        return jnp.where(first_core, vv * RING + uu, uu * RING + vv)

    def remote(src, dst, send, recv, core, wide, blk):
        return pltpu.make_async_remote_copy(
            src_ref=src,
            dst_ref=dst,
            send_sem=send,
            recv_sem=recv,
            device_id=(core, wide, blk),
            device_id_type=MESH,
        )

    sister = (1 - s, w, x)
    core_t = (y + z) % 2
    slot = w // 2

    def chip(core, m):
        return 2 * m + (core + m // 4) % 2

    own_target = core_t == s

    lead = pl.multiple_of(jnp.maximum(x * QUARTER - WPRE, 0), 32)
    here = pl.multiple_of(x * QUARTER, QUARTER)
    main_copy = pltpu.make_async_copy(
        weather.at[pl.ds(here, QUARTER)], wraw.at[pl.ds(WPRE, QUARTER)], loc_sem.at[0]
    )
    lead_copy = pltpu.make_async_copy(
        weather.at[pl.ds(lead, WPRE)], wraw.at[pl.ds(0, WPRE)], loc_sem.at[1]
    )
    resp_copy = pltpu.make_async_copy(resp, rraw, own_sem)
    resp_copy.start()
    main_copy.start()
    lead_copy.start()

    barrier = pltpu.get_barrier_semaphore()

    def greet(core, wide, blk):
        pl.semaphore_signal(barrier, inc=1, device_id=(core, wide, blk), device_id_type=MESH)

    greet(s, w, right)
    greet(s, w, left)
    greet(*sister)

    @pl.loop(1, RING)
    def _(step):
        greet(s, wide_of((u + step) % RING, v), x)

    greet(s, wide_of(u, (v + 1) % RING), x)
    greet(s, wide_of(u, (v + RING - 1) % RING), x)

    @pl.loop(1, HALF)
    def _(step):
        greet(core_t, chip(s, (slot + step) % HALF), x)

    @pl.when(jnp.logical_not(own_target))
    def _():
        greet(core_t, chip(s, slot), x)

    def lay_out(core):
        for lag in range(GROUP // 2):
            column = (lag % PIECE) * CH
            rbuf[4 * x + 2 * core + lag // PIECE, :, column : column + CH] = r32[
                pl.ds(GROUP // 2 * core + lag, BS, stride=GROUP), :
            ].astype(jnp.bfloat16)

    resp_copy.wait()
    r32[...] = rraw[...].astype(jnp.float32)
    lay_out(s)

    pl.semaphore_wait(barrier, 3 + RING - 1 + 2 + HALF - 1 + jnp.where(own_target, 0, 1))

    def a_copy(index, src, piece, blk):
        return remote(src, rbuf.at[piece], a_send.at[index], a_recv.at[index], s, w, blk)

    p0, p1 = 2 * s, 2 * s + 1
    a_copies = [
        a_copy(0, rbuf.at[4 * x + p0], 4 * x + p0, right),
        a_copy(1, rbuf.at[4 * x + p1], 4 * x + p1, left),
        a_copy(2, rbuf.at[4 * x + p1], 4 * x + p1, right),
        a_copy(3, rbuf.at[4 * x + p0], 4 * x + p0, left),
    ]
    for copy in a_copies:
        copy.start()

    @pl.when(own_target)
    def _():
        pltpu.make_async_copy(coupling.at[0], cown.at[4 * v], c1_recv.at[0]).start()
        for away, place in ((1, 1), (7, 0), (2, 2), (6, 1), (3, 3), (5, 2), (4, 3)):
            remote(
                coupling.at[0],
                cown.at[4 * v + place],
                c1_send,
                c1_recv.at[place],
                s,
                wide_of((u + away) % RING, v),
                x,
            ).start()

    def c_step(way, step, piece):
        if way == 0:
            row, to = (v + RING - step + 1) % RING, (v + 1) % RING
        else:
            row, to = (v + step - 1) % RING, (v + RING - 1) % RING
        part = cown.at[4 * row + piece]
        index = (way * 4 + step - 1) * 4 + piece
        return remote(part, part, c2_send, c2_recv.at[index], s, wide_of(u, to), x)

    def goes(way, step, piece):
        return step < 4 or (step == 4 and piece // 2 == way)

    def c_begin(*pieces):
        for piece in pieces:
            drain(cown.at[0], c1_recv.at[piece])
            for way in range(2):
                c_step(way, 1, piece).start()

    def c_arrive(step, *pieces):
        for piece in pieces:
            for way in range(2):
                if goes(way, step, piece):
                    c_step(way, step, piece).wait_recv()
                    if goes(way, step + 1, piece):
                        c_step(way, step + 1, piece).start()

    main_copy.wait()
    lead_copy.wait()

    @pl.when(x == 0)
    def _():
        wraw[pl.ds(0, WPRE), :] = jnp.zeros((WPRE, CH), jnp.bfloat16)

    w32[...] = wraw[...].astype(jnp.float32)

    def columns(first, last):
        for lag in range(first, last):
            xbuf[:, lag * CH : (lag + 1) * CH] = w32[GROUP - lag : GROUP - lag + XROWS, :].astype(
                jnp.bfloat16
            )

    columns(0, 8)
    c_begin(0)
    columns(8, 16)
    c_begin(1)

    def add_groups(groups, tile, first=False):
        total = None if first else acc[pl.ds(tile * TILE, TILE), :]
        for group in groups:
            start = pl.multiple_of((LAGS - GROUP) - GROUP * group + tile * TILE, 16)
            for piece in range(4):
                term = lax.dot_general(
                    xbuf[pl.ds(start, TILE), piece * PIECE * CH : (piece + 1) * PIECE * CH],
                    rbuf[4 * group + piece],
                    (((1,), (1,)), ((), ())),
                    preferred_element_type=jnp.float32,
                )
                total = term if total is None else total + term
        return total

    def add_far(core, tile):
        start = pl.multiple_of((LAGS - GROUP) - GROUP * far + tile * TILE, 16)
        total = acc[pl.ds(tile * TILE, TILE), :]
        for half in range(2):
            piece = 2 * core + half
            column = pl.multiple_of(piece * PIECE * CH, PIECE * CH)
            total = total + lax.dot_general(
                xbuf[pl.ds(start, TILE), pl.ds(column, PIECE * CH)],
                rbuf[4 * far + piece],
                (((1,), (1,)), ((), ())),
                preferred_element_type=jnp.float32,
            )
        return total

    def keep(tile, total):
        acc[pl.ds(tile * TILE, TILE), :] = total

    lay_out(1 - s)
    keep(0, add_groups([x], 0, True))
    keep(1, add_groups([x], 1, True))

    def mirror_piece(piece, group_sem):
        remote(
            rbuf.at[piece], rbuf.at[piece], am_send, am_recv.at[group_sem], *sister
        ).start()

    a_copies[0].wait_recv()
    fwd_right = a_copy(4, rbuf.at[4 * left + p0], 4 * left + p0, right)
    fwd_right.start()
    a_copies[1].wait_recv()
    fwd_left = a_copy(5, rbuf.at[4 * right + p1], 4 * right + p1, left)
    fwd_left.start()
    mirror_piece(4 * left + p0, 0)
    mirror_piece(4 * right + p1, 1)

    c_begin(2)
    c_arrive(1, 0)
    keep(2, add_groups([x], 2, True))
    c_begin(3)
    c_arrive(1, 1)
    a_copies[2].wait_recv()
    mirror_piece(4 * left + p1, 0)
    a_copies[3].wait_recv()
    mirror_piece(4 * right + p0, 1)
    c_arrive(1, 2, 3)
    c_arrive(2, 0)
    drain(rbuf.at[pl.ds(0, 2)], am_recv.at[0])
    drain(rbuf.at[pl.ds(0, 2)], am_recv.at[1])
    keep(0, add_groups([left, right], 0))
    c_arrive(2, 1)
    keep(1, add_groups([left, right], 1))
    c_arrive(2, 2)
    fwd_right.wait_recv()
    mirror_piece(4 * far + p0, 2)
    fwd_left.wait_recv()
    mirror_piece(4 * far + p1, 2)
    keep(2, add_groups([left, right], 2))
    for tile in range(3):
        keep(tile, add_far(s, tile))
    c_arrive(2, 3)
    drain(rbuf.at[pl.ds(0, 2)], am_recv.at[2])
    for tile in range(3):
        lext[pl.ds(tile * TILE, TILE), :] = add_far(1 - s, tile).astype(jnp.bfloat16)

    def b_copy(step):
        i = (slot + STRIDE * step) % HALF
        return remote(
            lext.at[pl.ds(pl.multiple_of(ROWS * i, ROWS), LROWS)],
            lbuf.at[HALF * core_t + slot],
            b_send,
            b_recv.at[slot // 8],
            core_t,
            chip(s, i),
            x,
        )

    @pl.when(own_target)
    def _():
        pltpu.make_async_copy(
            lext.at[pl.ds(pl.multiple_of(ROWS * slot, ROWS), LROWS)],
            lbuf.at[HALF * core_t + slot],
            b_recv.at[slot // 8],
        ).start()

    @pl.when(jnp.logical_not(own_target))
    def _():
        b_copy(0).start()

    @pl.loop(1, HALF)
    def _(step):
        b_copy(step).start()

    c_arrive(3, 0, 1, 2, 3)

    mine = HALF * s
    theirs = HALF * (1 - s)

    def mirror(buf, first, count, send, recv):
        part = buf.at[pl.ds(first, count)]
        return remote(part, part, send, recv, *sister)

    def widen(first):
        l32[pl.ds(first, 8)] = lbuf[pl.ds(first, 8)].astype(jnp.float32)

    for part in range(4):
        drain(lbuf.at[pl.ds(0, 8)], b_recv.at[part])
        mirror(lbuf, mine + 8 * part, 8, bm_send, bm_recv.at[part]).start()
    c_arrive(4, 0, 2, 1, 3)
    for part in range(4):
        widen(mine + 8 * part)
    for part in range(4):
        drain(lbuf.at[pl.ds(0, 8)], bm_recv.at[part])
        widen(theirs + 8 * part)

    def block_of(wide):
        return HALF * ((wide // RING + wide) % 2) + wide // 2

    def moved(series, m, start, rows):
        wide = chip(s, m)
        upstream = [
            series[block_of(sources[k, wide]), pl.ds(start - delays[k, wide], rows), :]
            for k in range(2)
        ]
        lhs = jnp.concatenate(upstream, axis=1).astype(jnp.bfloat16)
        wy, wz = wide // RING, wide % RING
        row = jnp.where(first_core, wy, wz)
        away = (jnp.where(first_core, wz, wy) - u + RING) % RING
        place = jnp.where(
            away % 2 == 0,
            jnp.where(away == 0, 0, jnp.where(away == 2, 1, jnp.where(away == 6, 2, 3))),
            jnp.where(away == 1, 0, jnp.where(away == 7, 1, jnp.where(away == 3, 2, 3))),
        )
        rhs = cown[4 * row + place].reshape(2 * BS, BS)
        return jnp.dot(lhs, rhs, preferred_element_type=jnp.float32)

    for part in range(4):

        @pl.loop(0, 8, unroll=8)
        def _(m):
            i = mine + 8 * part + m
            total = l32[i, HALO:LROWS, :] + moved(l32, 8 * part + m, HALO, FROWS)
            rounded = total.astype(jnp.bfloat16)
            fbuf[i] = rounded
            f32b[i] = rounded.astype(jnp.float32)

        mirror(fbuf, mine + 8 * part, 8, f_send, f_recv.at[part]).start()

    for part in range(4):
        drain(fbuf.at[pl.ds(0, 8)], f_recv.at[part])
        f32b[pl.ds(theirs + 8 * part, 8)] = fbuf[pl.ds(theirs + 8 * part, 8)].astype(jnp.float32)

    span = pl.ds(pl.multiple_of(ROWS * slot, ROWS), ROWS)

    def second(m):
        i = mine + m
        total = f32b[i, HALO:FROWS, :] + moved(f32b, m, HALO, ROWS)
        sbuf[m] = total.astype(jnp.bfloat16)

    def e_copy(m):
        return remote(sbuf.at[m], out.at[span], e_send, e_recv, core_t, chip(s, m), x)

    def e_local():
        return pltpu.make_async_copy(sbuf.at[slot], out.at[span], e_recv)

    @pl.loop(0, 4)
    def _(column):
        for row in (s, 1 - s):
            picked = [4 * (row + 2 * ((y // 2 + k) % 4)) + column for k in range(4)]
            for m in picked:
                second(m)
            for k, m in enumerate(picked):
                if k > 0:
                    e_copy(m).start()
                    continue
                stays = jnp.logical_and(own_target, m == slot)

                @pl.when(stays)
                def _():
                    e_local().start()

                @pl.when(jnp.logical_not(stays))
                def _():
                    e_copy(m).start()

    drain(out, e_recv)
    for copy in a_copies + [fwd_right, fwd_left]:
        copy.wait_send()
    drain(rbuf.at[pl.ds(0, 6)], am_send)
    drain(cown.at[pl.ds(0, 28)], c2_send)

    @pl.when(own_target)
    def _():
        drain(cown.at[pl.ds(0, RING - 1)], c1_send)

    drain(lbuf.at[pl.ds(0, HALF - 1)], b_send)
    drain(sbuf.at[pl.ds(0, HALF - 1)], e_send)

    @pl.when(jnp.logical_not(own_target))
    def _():
        drain(lbuf.at[0], b_send)
        drain(sbuf.at[0], e_send)

    drain(lbuf.at[pl.ds(0, HALF)], bm_send)
    drain(fbuf.at[pl.ds(0, HALF)], f_send)


def body(weather, response, coupling, sources, delays):
    rows_of_lags = response.reshape(BS * GROUP, CH)
    bf16, f32 = jnp.bfloat16, jnp.float32
    vm, dma = pltpu.VMEM, pltpu.SemaphoreType.DMA
    rows = pl.pallas_call(
        kernel,
        out_shape=jax.ShapeDtypeStruct((QUARTER, BS), bf16),
        in_specs=[pl.BlockSpec(memory_space=pltpu.HBM)] * 3
        + [pl.BlockSpec(memory_space=pltpu.SMEM)] * 2,
        out_specs=pl.BlockSpec(memory_space=pl.ANY),
        scratch_shapes=[
            vm((BS * GROUP, CH), bf16),
            vm((BS * GROUP, CH), f32),
            vm((WPRE + QUARTER, CH), bf16),
            vm((WPRE + QUARTER, CH), f32),
            vm((XROWS, GROUP * CH), bf16),
            vm((16, BS, PIECE * CH), bf16),
            vm((EXT, BS), f32),
            vm((EXT, BS), bf16),
            vm((BLOCKS, LROWS, BS), bf16),
            vm((BLOCKS, LROWS, BS), f32),
            vm((BLOCKS, FROWS, BS), bf16),
            vm((BLOCKS, FROWS, BS), f32),
            vm((HALF, ROWS, BS), bf16),
            vm((HALF, 2, BS, BS), bf16),
            dma((2,)),
            dma,
            dma((6,)),
            dma((6,)),
            dma,
            dma((3,)),
            dma,
            dma((4,)),
            dma,
            dma((32,)),
            dma,
            dma((4,)),
            dma,
            dma((4,)),
            dma,
            dma((4,)),
            dma,
            dma,
        ],
        compiler_params=pltpu.CompilerParams(
            collective_id=0, has_side_effects=True, vmem_limit_bytes=60 * 1024 * 1024
        ),
    )(weather, rows_of_lags, coupling, sources.T, delays.T)
    return rows.T


def solution(mesh):
    placed = (P("scen", None), P("wide", "blk", None), P("wide", None, None, None), P(), P())
    return jax.shard_map(
        body, mesh=mesh, in_specs=placed, out_specs=P(("scen", "wide"), "blk"), check_vma=False
    )
```

```python
import functools

import jax
import jax.numpy as jnp
from jax import lax
from jax.experimental import pallas as pl
from jax.experimental.pallas import tpu as pltpu
from jax.sharding import PartitionSpec as P

MESH = pl.DeviceIdType.MESH
CH = 128
LAGS = 64
BS = 128
HALO = 16
RING = 8
BLOCKS = 64
HALF = 32
ROWS = 32
QUARTER = HALF * ROWS
EXT = QUARTER + 2 * HALO
LROWS = ROWS + 2 * HALO
FROWS = ROWS + HALO
PIECE = 4
PARTS = 4
GROUP = 16
XROWS = EXT + LAGS - GROUP
WPRE = 96
TILE = 352
STRIDE = 5


def drain(ref, sem):
    pltpu.make_async_copy(ref, ref, sem).wait()


def kernel(
    weather,
    resp,
    coupling,
    sources,
    delays,
    out,
    rraw,
    r32,
    wraw,
    w32,
    xbuf,
    rbuf,
    acc,
    lext,
    lbuf,
    l32,
    fbuf,
    f32b,
    sbuf,
    cown,
    loc_sem,
    own_sem,
    a_send,
    a_recv,
    am_send,
    am_recv,
    c1_send,
    c1_recv,
    c2_send,
    c2_recv,
    b_send,
    b_recv,
    bm_send,
    bm_recv,
    f_send,
    f_recv,
    e_send,
    e_recv,
):
    s = lax.axis_index("scen")
    w = lax.axis_index("wide")
    x = lax.axis_index("blk")
    y, z = w // RING, w % RING
    first_core = s == 0
    u = jnp.where(first_core, z, y)
    v = jnp.where(first_core, y, z)
    right, left = (x + 1) % PARTS, (x + PARTS - 1) % PARTS
    far = (x + 2) % PARTS

    def wide_of(uu, vv):
        return jnp.where(first_core, vv * RING + uu, uu * RING + vv)

    def remote(src, dst, send, recv, core, wide, blk):
        return pltpu.make_async_remote_copy(
            src_ref=src,
            dst_ref=dst,
            send_sem=send,
            recv_sem=recv,
            device_id=(core, wide, blk),
            device_id_type=MESH,
        )

    sister = (1 - s, w, x)
    core_t = (y + z) % 2
    slot = w // 2

    def chip(core, m):
        return 2 * m + (core + m // 4) % 2

    own_target = core_t == s

    lead = pl.multiple_of(jnp.maximum(x * QUARTER - WPRE, 0), 32)
    here = pl.multiple_of(x * QUARTER, QUARTER)
    main_copy = pltpu.make_async_copy(
        weather.at[pl.ds(here, QUARTER)], wraw.at[pl.ds(WPRE, QUARTER)], loc_sem.at[0]
    )
    lead_copy = pltpu.make_async_copy(
        weather.at[pl.ds(lead, WPRE)], wraw.at[pl.ds(0, WPRE)], loc_sem.at[1]
    )
    resp_copy = pltpu.make_async_copy(resp, rraw, own_sem)
    resp_copy.start()
    main_copy.start()
    lead_copy.start()

    barrier = pltpu.get_barrier_semaphore()

    def greet(core, wide, blk):
        pl.semaphore_signal(barrier, inc=1, device_id=(core, wide, blk), device_id_type=MESH)

    greet(s, w, right)
    greet(s, w, left)
    greet(*sister)

    @pl.loop(1, RING)
    def _(step):
        greet(s, wide_of((u + step) % RING, v), x)

    greet(s, wide_of(u, (v + 1) % RING), x)
    greet(s, wide_of(u, (v + RING - 1) % RING), x)

    @pl.loop(1, HALF)
    def _(step):
        greet(core_t, chip(s, (slot + step) % HALF), x)

    @pl.when(jnp.logical_not(own_target))
    def _():
        greet(core_t, chip(s, slot), x)

    def lay_out(core):
        for lag in range(GROUP // 2):
            column = (lag % PIECE) * CH
            rbuf[4 * x + 2 * core + lag // PIECE, :, column : column + CH] = r32[
                pl.ds(GROUP // 2 * core + lag, BS, stride=GROUP), :
            ].astype(jnp.bfloat16)

    resp_copy.wait()
    r32[...] = rraw[...].astype(jnp.float32)
    lay_out(s)

    pl.semaphore_wait(barrier, 3 + RING - 1 + 2 + HALF - 1 + jnp.where(own_target, 0, 1))

    def a_copy(index, src, piece, blk):
        return remote(src, rbuf.at[piece], a_send.at[index], a_recv.at[index], s, w, blk)

    p0, p1 = 2 * s, 2 * s + 1
    a_copies = [
        a_copy(0, rbuf.at[4 * x + p0], 4 * x + p0, right),
        a_copy(1, rbuf.at[4 * x + p1], 4 * x + p1, left),
        a_copy(2, rbuf.at[4 * x + p1], 4 * x + p1, right),
        a_copy(3, rbuf.at[4 * x + p0], 4 * x + p0, left),
    ]
    for copy in a_copies:
        copy.start()

    @pl.when(own_target)
    def _():
        pltpu.make_async_copy(coupling.at[0], cown.at[4 * v], c1_recv.at[0]).start()
        for away, place in ((1, 1), (7, 0), (2, 2), (6, 1), (3, 3), (5, 2), (4, 3)):
            remote(
                coupling.at[0],
                cown.at[4 * v + place],
                c1_send,
                c1_recv.at[place],
                s,
                wide_of((u + away) % RING, v),
                x,
            ).start()

    def c_step(way, step, piece):
        if way == 0:
            row, to = (v + RING - step + 1) % RING, (v + 1) % RING
        else:
            row, to = (v + step - 1) % RING, (v + RING - 1) % RING
        part = cown.at[4 * row + piece]
        index = (way * 4 + step - 1) * 4 + piece
        return remote(part, part, c2_send, c2_recv.at[index], s, wide_of(u, to), x)

    def goes(way, step, piece):
        return step < 4 or (step == 4 and piece // 2 == way)

    def c_begin(*pieces):
        for piece in pieces:
            drain(cown.at[0], c1_recv.at[piece])
            for way in range(2):
                c_step(way, 1, piece).start()

    def c_arrive(step, *pieces):
        for piece in pieces:
            for way in range(2):
                if goes(way, step, piece):
                    c_step(way, step, piece).wait_recv()
                    if goes(way, step + 1, piece):
                        c_step(way, step + 1, piece).start()

    main_copy.wait()
    lead_copy.wait()

    @pl.when(x == 0)
    def _():
        wraw[pl.ds(0, WPRE), :] = jnp.zeros((WPRE, CH), jnp.bfloat16)

    w32[...] = wraw[...].astype(jnp.float32)

    def columns(first, last):
        for lag in range(first, last):
            xbuf[:, lag * CH : (lag + 1) * CH] = w32[GROUP - lag : GROUP - lag + XROWS, :].astype(
                jnp.bfloat16
            )

    columns(0, 8)
    c_begin(0)
    columns(8, 16)
    c_begin(1)

    def add_groups(groups, tile, first=False):
        total = None if first else acc[pl.ds(tile * TILE, TILE), :]
        for group in groups:
            start = pl.multiple_of((LAGS - GROUP) - GROUP * group + tile * TILE, 16)
            for piece in range(4):
                term = lax.dot_general(
                    xbuf[pl.ds(start, TILE), piece * PIECE * CH : (piece + 1) * PIECE * CH],
                    rbuf[4 * group + piece],
                    (((1,), (1,)), ((), ())),
                    preferred_element_type=jnp.float32,
                )
                total = term if total is None else total + term
        return total

    def add_far(core, tile):
        start = pl.multiple_of((LAGS - GROUP) - GROUP * far + tile * TILE, 16)
        total = acc[pl.ds(tile * TILE, TILE), :]
        for half in range(2):
            piece = 2 * core + half
            column = pl.multiple_of(piece * PIECE * CH, PIECE * CH)
            total = total + lax.dot_general(
                xbuf[pl.ds(start, TILE), pl.ds(column, PIECE * CH)],
                rbuf[4 * far + piece],
                (((1,), (1,)), ((), ())),
                preferred_element_type=jnp.float32,
            )
        return total

    def keep(tile, total):
        acc[pl.ds(tile * TILE, TILE), :] = total

    lay_out(1 - s)
    keep(0, add_groups([x], 0, True))
    keep(1, add_groups([x], 1, True))

    def mirror_piece(piece, group_sem):
        remote(
            rbuf.at[piece], rbuf.at[piece], am_send, am_recv.at[group_sem], *sister
        ).start()

    a_copies[0].wait_recv()
    fwd_right = a_copy(4, rbuf.at[4 * left + p0], 4 * left + p0, right)
    fwd_right.start()
    a_copies[1].wait_recv()
    fwd_left = a_copy(5, rbuf.at[4 * right + p1], 4 * right + p1, left)
    fwd_left.start()
    mirror_piece(4 * left + p0, 0)
    mirror_piece(4 * right + p1, 1)

    c_begin(2)
    c_arrive(1, 0)
    keep(2, add_groups([x], 2, True))
    c_begin(3)
    c_arrive(1, 1)
    a_copies[2].wait_recv()
    mirror_piece(4 * left + p1, 0)
    a_copies[3].wait_recv()
    mirror_piece(4 * right + p0, 1)
    c_arrive(1, 2, 3)
    c_arrive(2, 0)
    drain(rbuf.at[pl.ds(0, 2)], am_recv.at[0])
    drain(rbuf.at[pl.ds(0, 2)], am_recv.at[1])
    keep(0, add_groups([left, right], 0))
    c_arrive(2, 1)
    keep(1, add_groups([left, right], 1))
    c_arrive(2, 2)
    fwd_right.wait_recv()
    mirror_piece(4 * far + p0, 2)
    fwd_left.wait_recv()
    mirror_piece(4 * far + p1, 2)
    keep(2, add_groups([left, right], 2))
    for tile in range(3):
        keep(tile, add_far(s, tile))
    c_arrive(2, 3)
    drain(rbuf.at[pl.ds(0, 2)], am_recv.at[2])
    for tile in range(3):
        lext[pl.ds(tile * TILE, TILE), :] = add_far(1 - s, tile).astype(jnp.bfloat16)

    def b_copy(step):
        i = (slot + STRIDE * step) % HALF
        return remote(
            lext.at[pl.ds(pl.multiple_of(ROWS * i, ROWS), LROWS)],
            lbuf.at[HALF * core_t + slot],
            b_send,
            b_recv.at[slot // 8],
            core_t,
            chip(s, i),
            x,
        )

    @pl.when(own_target)
    def _():
        pltpu.make_async_copy(
            lext.at[pl.ds(pl.multiple_of(ROWS * slot, ROWS), LROWS)],
            lbuf.at[HALF * core_t + slot],
            b_recv.at[slot // 8],
        ).start()

    @pl.when(jnp.logical_not(own_target))
    def _():
        b_copy(0).start()

    @pl.loop(1, HALF)
    def _(step):
        b_copy(step).start()

    c_arrive(3, 0, 1, 2, 3)
    c_arrive(4, 0, 2, 1, 3)

    mine = HALF * s
    theirs = HALF * (1 - s)

    def mirror(buf, first, count, send, recv):
        part = buf.at[pl.ds(first, count)]
        return remote(part, part, send, recv, *sister)

    def widen(first):
        l32[pl.ds(first, 8)] = lbuf[pl.ds(first, 8)].astype(jnp.float32)

    for part in range(4):
        drain(lbuf.at[pl.ds(0, 8)], b_recv.at[part])
        mirror(lbuf, mine + 8 * part, 8, bm_send, bm_recv.at[part]).start()
    for part in range(4):
        widen(mine + 8 * part)
    for part in range(4):
        drain(lbuf.at[pl.ds(0, 8)], bm_recv.at[part])
        widen(theirs + 8 * part)

    def block_of(wide):
        return HALF * ((wide // RING + wide) % 2) + wide // 2

    def moved(series, m, start, rows):
        wide = chip(s, m)
        upstream = [
            series[block_of(sources[k, wide]), pl.ds(start - delays[k, wide], rows), :]
            for k in range(2)
        ]
        lhs = jnp.concatenate(upstream, axis=1).astype(jnp.bfloat16)
        wy, wz = wide // RING, wide % RING
        row = jnp.where(first_core, wy, wz)
        away = (jnp.where(first_core, wz, wy) - u + RING) % RING
        place = jnp.where(
            away % 2 == 0,
            jnp.where(away == 0, 0, jnp.where(away == 2, 1, jnp.where(away == 6, 2, 3))),
            jnp.where(away == 1, 0, jnp.where(away == 7, 1, jnp.where(away == 3, 2, 3))),
        )
        rhs = cown[4 * row + place].reshape(2 * BS, BS)
        return jnp.dot(lhs, rhs, preferred_element_type=jnp.float32)

    for part in range(4):

        @pl.loop(0, 8, unroll=8)
        def _(m):
            i = mine + 8 * part + m
            total = l32[i, HALO:LROWS, :] + moved(l32, 8 * part + m, HALO, FROWS)
            rounded = total.astype(jnp.bfloat16)
            fbuf[i] = rounded
            f32b[i] = rounded.astype(jnp.float32)

        mirror(fbuf, mine + 8 * part, 8, f_send, f_recv.at[part]).start()

    for part in range(4):
        drain(fbuf.at[pl.ds(0, 8)], f_recv.at[part])
        f32b[pl.ds(theirs + 8 * part, 8)] = fbuf[pl.ds(theirs + 8 * part, 8)].astype(jnp.float32)

    span = pl.ds(pl.multiple_of(ROWS * slot, ROWS), ROWS)

    def second(m):
        i = mine + m
        total = f32b[i, HALO:FROWS, :] + moved(f32b, m, HALO, ROWS)
        sbuf[m] = total.astype(jnp.bfloat16)

    def e_copy(m):
        return remote(sbuf.at[m], out.at[span], e_send, e_recv, core_t, chip(s, m), x)

    def e_local():
        return pltpu.make_async_copy(sbuf.at[slot], out.at[span], e_recv)

    @pl.loop(0, 4)
    def _(column):
        for row in (s, 1 - s):
            picked = [4 * (row + 2 * ((y // 2 + k) % 4)) + column for k in range(4)]
            for k, m in enumerate(picked):
                if k % 2 == 0:
                    second(m)
                    second(picked[k + 1])
                if k > 0:
                    e_copy(m).start()
                    continue
                stays = jnp.logical_and(own_target, m == slot)

                @pl.when(stays)
                def _():
                    e_local().start()

                @pl.when(jnp.logical_not(stays))
                def _():
                    e_copy(m).start()

    drain(out, e_recv)
    for copy in a_copies + [fwd_right, fwd_left]:
        copy.wait_send()
    drain(rbuf.at[pl.ds(0, 6)], am_send)
    drain(cown.at[pl.ds(0, 28)], c2_send)

    @pl.when(own_target)
    def _():
        drain(cown.at[pl.ds(0, RING - 1)], c1_send)

    drain(lbuf.at[pl.ds(0, HALF - 1)], b_send)
    drain(sbuf.at[pl.ds(0, HALF - 1)], e_send)

    @pl.when(jnp.logical_not(own_target))
    def _():
        drain(lbuf.at[0], b_send)
        drain(sbuf.at[0], e_send)

    drain(lbuf.at[pl.ds(0, HALF)], bm_send)
    drain(fbuf.at[pl.ds(0, HALF)], f_send)


def body(weather, response, coupling, sources, delays):
    rows_of_lags = response.reshape(BS * GROUP, CH)
    bf16, f32 = jnp.bfloat16, jnp.float32
    vm, dma = pltpu.VMEM, pltpu.SemaphoreType.DMA
    rows = pl.pallas_call(
        kernel,
        out_shape=jax.ShapeDtypeStruct((QUARTER, BS), bf16),
        in_specs=[pl.BlockSpec(memory_space=pltpu.HBM)] * 3
        + [pl.BlockSpec(memory_space=pltpu.SMEM)] * 2,
        out_specs=pl.BlockSpec(memory_space=pl.ANY),
        scratch_shapes=[
            vm((BS * GROUP, CH), bf16),
            vm((BS * GROUP, CH), f32),
            vm((WPRE + QUARTER, CH), bf16),
            vm((WPRE + QUARTER, CH), f32),
            vm((XROWS, GROUP * CH), bf16),
            vm((16, BS, PIECE * CH), bf16),
            vm((EXT, BS), f32),
            vm((EXT, BS), bf16),
            vm((BLOCKS, LROWS, BS), bf16),
            vm((BLOCKS, LROWS, BS), f32),
            vm((BLOCKS, FROWS, BS), bf16),
            vm((BLOCKS, FROWS, BS), f32),
            vm((HALF, ROWS, BS), bf16),
            vm((HALF, 2, BS, BS), bf16),
            dma((2,)),
            dma,
            dma((6,)),
            dma((6,)),
            dma,
            dma((3,)),
            dma,
            dma((4,)),
            dma,
            dma((32,)),
            dma,
            dma((4,)),
            dma,
            dma((4,)),
            dma,
            dma((4,)),
            dma,
            dma,
        ],
        compiler_params=pltpu.CompilerParams(
            collective_id=0, has_side_effects=True, vmem_limit_bytes=60 * 1024 * 1024
        ),
    )(weather, rows_of_lags, coupling, sources.T, delays.T)
    return rows.T


def solution(mesh):
    placed = (P("scen", None), P("wide", "blk", None), P("wide", None, None, None), P(), P())
    return jax.shard_map(
        body, mesh=mesh, in_specs=placed, out_specs=P(("scen", "wide"), "blk"), check_vma=False
    )
```
